32 devices in a mesh: dp: 8 (over y, x, core), fsdp: 4 (over z).
Axes of the slice: x: 2, y: 2, z: 4, core: 2. Of those that a mesh axis runs over, the one named last changes fastest.
Arguments:
- tokens: bfloat16 [32768, 1024], P(('dp', 'fsdp')), may hold values from -6 to 6
- segments: int32 [32768], P(('dp', 'fsdp')), may hold values from 0 to 127, never falling along the last dimension, each value on 1 to 1024 neighbouring positions
- cotangent: bfloat16 [32768, 1024], P(('dp', 'fsdp')), may hold values from -16 to 16
- ln1_gain: bfloat16 [1024], P(('dp', 'fsdp')), may hold values from 0.5 to 1.5
- ln1_bias: bfloat16 [1024], P(('dp', 'fsdp')), may hold values from -1.5 to 1.5
- w_qkv: bfloat16 [1024, 3072], P(('dp', 'fsdp')), may hold values from -0.1875 to 0.1875
- b_qkv: bfloat16 [3072], P(('dp', 'fsdp')), may hold values from -1.5 to 1.5
- w_out: bfloat16 [1024, 1024], P(('dp', 'fsdp')), may hold values from -0.75 to 0.75
- b_out: bfloat16 [1024], P(('dp', 'fsdp')), may hold values from -1.5 to 1.5
- ln2_gain: bfloat16 [1024], P(('dp', 'fsdp')), may hold values from 0.5 to 1.5
- ln2_bias: bfloat16 [1024], P(('dp', 'fsdp')), may hold values from -1.5 to 1.5
- w_fc: bfloat16 [1024, 4096], P(('dp', 'fsdp')), may hold values from -0.1875 to 0.1875
- b_fc: bfloat16 [4096], P(('dp', 'fsdp')), may hold values from -1.5 to 1.5
- w_proj: bfloat16 [4096, 1024], P(('dp', 'fsdp')), may hold values from -0.09375 to 0.09375
- b_proj: bfloat16 [1024], P(('dp', 'fsdp')), may hold values from -1.5 to 1.5
- prefix_embed: bfloat16 [10, 1024], replicated, may hold values from -6 to 6
- w_mid: bfloat16 [1024, 512], replicated, may hold values from -0.1875 to 0.1875
- b_mid: bfloat16 [512], replicated, may hold values from -1.5 to 1.5
- w_kv: bfloat16 [512, 2048], replicated, may hold values from -0.25 to 0.25
- b_kv: bfloat16 [2048], replicated, may hold values from -1.5 to 1.5
Outputs:
- block_out: bfloat16 [32768, 1024], P(('dp', 'fsdp'))
- grad_tokens: bfloat16 [32768, 1024], P(('dp', 'fsdp'))
- grad_embed: float32 [10, 1024], replicated
- grad_mid_w: float32 [1024, 512], replicated
- grad_mid_b: float32 [512], replicated
- grad_kv_w: float32 [512, 2048], replicated
- grad_kv_b: float32 [2048], replicated
The draws below stay inside these ranges and needn't reach their ends.
Inputs may be any that keep to these rules, and one draw needn't show every extreme that they name: `segments`: segment numbers never fall along the tokens, every number up to the largest occurs, each covers 1 to 1024 tokens and some number exactly 1024; a number may continue across two sequences.
All inputs are finite; a program needn't handle non-finite values.
Results may differ from the reference program's by a relative error of at most 0.013.
Values may be sent and summed in bfloat16 or wider, within the bound.
No kernel may reach another device: no remote copies, remote signals or barrier semaphores. Data moves between devices by JAX's collectives and lax.ppermute only.
A program may use at most 192 MiB of HBM per device.

```python
import math
import jax
import jax.numpy as jnp
import numpy as np
from jax import lax

D = 1024
FF = 4096
HEAD = 64
MIDDLE = 512
PREFIX = 10
LENGTH = 1024
HEADS = 16
SEQUENCES = 32
TOKENS = 32768


def draw_cotangent(key, part):
    key = jax.random.fold_in(key, 7)
    positions = jnp.arange(TOKENS, dtype=jnp.float32) / TOKENS
    random_part = jnp.clip(jax.random.normal(key, (TOKENS, D), jnp.float32), -4.0, 4.0)
    row_scale = 1.0 + 2.0 * positions
    return (random_part * row_scale[:, None]).astype(jnp.bfloat16)


def steps_of(stream_key, shape, pieces, smallest, high):
    gain = 1.0
    for dim, blocks in pieces:
        draws = jax.random.uniform(jax.random.fold_in(jax.random.fold_in(stream_key, 6), dim), (blocks,), jnp.float32, smallest / len(pieces), high / len(pieces))
        gain = gain * jnp.repeat(jnp.exp(draws), shape[dim] // blocks).reshape((-1,) + (1,) * (len(shape) - 1 - dim))
    return gain


def split_up(number_of, total, bound, skew):
    portions = [(1 << 20) // math.isqrt(standing ** skew) + 1 for standing in range(2, number_of + 1)]
    surplus, holding = total - bound - (number_of - 1), [1] * (number_of - 1)
    while surplus > 0:
        candidates = [i for i in range(number_of - 1) if holding[i] < bound]
        pool, budget = sum([portions[i] for i in candidates]), surplus
        for i in candidates:
            more = min(bound - holding[i], max(1, budget * portions[i] // pool), surplus)
            holding[i] = holding[i] + more
            surplus = surplus - more
    return np.array([bound] + holding)


def uneven_parts(own_key, count, total, reach, lean):
    if count == 2:
        one = jax.random.randint(own_key, (), max(1, total - reach), min(reach, total - 1) + 1)
        return jnp.stack([one, total - one])
    tallies = jnp.asarray(split_up(count, total, reach, lean), jnp.int32)
    pairs = (count - 1) // 2
    giver, sink = tallies[1:1 + 2 * pairs:2], tallies[2:2 + 2 * pairs:2]
    margin = jnp.minimum(giver - 1, reach - sink)
    shifted = jax.random.randint(jax.random.fold_in(own_key, 1), (pairs,), 0, 1 << 20) % (margin + 1)
    tallies = tallies.at[1:1 + 2 * pairs:2].set(giver - shifted).at[2:2 + 2 * pairs:2].set(sink + shifted)
    return tallies[jax.random.permutation(jax.random.fold_in(own_key, 2), count)]


def bell_draw(key, dims, scale, most, shards=(), kind=jnp.bfloat16):
    values = jax.random.normal(key, dims, jnp.float32) * scale
    if len(shards) > 0:
        values = steps_of(key, dims, shards, -0.22, 0.18) * values
    return jnp.clip(values, min=-most, max=most).astype(kind)


def setup_inputs(seed: int = 0) -> dict:
    key_list = jax.random.split(jax.random.key(seed), 21)
    return {
        "tokens": bell_draw(key_list[0], (TOKENS, D), 1.0, 6.0, ((0, 32),)),
        "segments": jnp.searchsorted(jnp.cumsum(uneven_parts(key_list[1], TOKENS * 4 // LENGTH, TOKENS, LENGTH, 2)), jnp.arange(TOKENS), side="right").astype(jnp.int32),
        "cotangent": draw_cotangent(jax.random.fold_in(key_list[20], 71), 0),
        "ln1_gain": jnp.clip(1.0 + 0.1 * jax.random.normal(key_list[3], (D,), jnp.float32), 0.5, 1.5).astype(jnp.bfloat16),
        "ln1_bias": bell_draw(key_list[4], (D,), 0.3, 1.5, ((0, 32),)),
        "w_qkv": bell_draw(key_list[5], (D, 3 * D), D ** -0.5, 0.1875, ((0, 32),)),
        "b_qkv": bell_draw(key_list[6], (3 * D,), 0.3, 1.5, ((0, 32),)),
        "w_out": bell_draw(key_list[7], (D, D), (D // 16) ** -0.5, 0.75, ((0, 32),)),
        "b_out": bell_draw(key_list[8], (D,), 0.3, 1.5, ((0, 32),)),
        "ln2_gain": jnp.clip(1.0 + 0.1 * jax.random.normal(key_list[9], (D,), jnp.float32), 0.5, 1.5).astype(jnp.bfloat16),
        "ln2_bias": bell_draw(key_list[10], (D,), 0.3, 1.5, ((0, 32),)),
        "w_fc": bell_draw(key_list[11], (D, FF), D ** -0.5, 0.1875, ((0, 32),)),
        "b_fc": bell_draw(key_list[12], (FF,), 0.3, 1.5, ((0, 32),)),
        "w_proj": bell_draw(key_list[13], (FF, D), FF ** -0.5, 0.09375, ((0, 32),)),
        "b_proj": bell_draw(key_list[14], (D,), 0.3, 1.5, ((0, 32),)),
        "prefix_embed": bell_draw(key_list[15], (PREFIX, D), 1.0, 6.0),
        "w_mid": bell_draw(key_list[16], (D, MIDDLE), D ** -0.5, 0.1875),
        "b_mid": bell_draw(key_list[17], (MIDDLE,), 0.3, 1.5),
        "w_kv": bell_draw(key_list[18], (MIDDLE, 2 * D), MIDDLE ** -0.5, 0.25),
        "b_kv": bell_draw(key_list[19], (2 * D,), 0.3, 1.5),
    }


@jax.custom_vjp
def low(v):
    return lax.optimization_barrier(v.astype(jnp.bfloat16)).astype(jnp.float32)

@jax.custom_vjp
def low_back(v):
    return v

def low_keep(v):
    return (low(v), None)

def low_pass(kept, grad):
    return (grad,)

def back_keep(v):
    return (v, None)

def back_low(kept, grad):
    return (low(grad),)
low.defvjp(low_keep, low_pass)
low_back.defvjp(back_keep, back_low)

def layer_norm(values, gain_row, shift_row):
    row_mean = lax.optimization_barrier(jnp.mean(values, axis=-1, keepdims=True))
    centred = values - row_mean
    spread = lax.optimization_barrier(jnp.mean(centred * centred, axis=-1, keepdims=True))
    return centred * lax.rsqrt(spread + 1e-05) * gain_row + shift_row

def matmul(left, right):
    return jnp.dot(left, right, precision=lax.Precision.HIGHEST)

def sequence_block(seq_input, segment_row, prefix_key, prefix_value, frozen):
    gain_one, shift_one, qkv_weight, qkv_bias, out_weight, out_bias, gain_two, shift_two, fc_weight, fc_bias, proj_weight, proj_bias = frozen
    highest = lax.Precision.HIGHEST
    normed = layer_norm(seq_input, gain_one, shift_one)
    qkv = low(low_back(matmul(low(normed), qkv_weight) + qkv_bias))
    queries = qkv[:, :D].reshape(LENGTH, HEADS, HEAD)
    key_all = jnp.concatenate([prefix_key, qkv[:, D:2 * D]], 0).reshape(PREFIX + LENGTH, HEADS, HEAD)
    value_all = jnp.concatenate([prefix_value, qkv[:, 2 * D:]], 0).reshape(PREFIX + LENGTH, HEADS, HEAD)
    scores = jnp.einsum('qhe,khe->hqk', queries, key_all, precision=highest) * HEAD ** (-0.5)
    scores = low_back(scores)
    places = jnp.arange(LENGTH)
    seen_tok = (segment_row[:, None] == segment_row[None, :]) & (places[:, None] >= places[None, :])
    seen_all = jnp.concatenate([jnp.ones((LENGTH, PREFIX), dtype=jnp.bool_), seen_tok], 1)
    scores = jnp.where(seen_all[None], scores, -1e+30)
    probs = low(jax.nn.softmax(scores, axis=-1))
    hidden = jnp.einsum('hqk,khe->qhe', probs, value_all, precision=highest).reshape(LENGTH, D)
    hidden = low(low_back(hidden))
    mixed = seq_input + low_back(matmul(hidden, out_weight) + out_bias)
    normed_two = layer_norm(mixed, gain_two, shift_two)
    pre_act = low_back(matmul(low(normed_two), fc_weight) + fc_bias)
    act = low(jax.nn.gelu(pre_act, approximate=True))
    return mixed + low_back(matmul(act, proj_weight) + proj_bias)

def reference(tokens, segments, cotangent, ln1_gain, ln1_bias, w_qkv, b_qkv, w_out, b_out, ln2_gain, ln2_bias, w_fc, b_fc, w_proj, b_proj, prefix_embed, w_mid, b_mid, w_kv, b_kv):
    frozen = tuple((member.astype(jnp.float32) for member in (ln1_gain, ln1_bias, w_qkv, b_qkv, w_out, b_out, ln2_gain, ln2_bias, w_fc, b_fc, w_proj, b_proj)))
    segment_rows = segments.reshape(SEQUENCES, LENGTH).astype(jnp.int32)

    def forward(all_input, embed, mid_weight, mid_bias, kv_weight, kv_bias):
        mid = jnp.tanh(low_back(matmul(embed, mid_weight) + mid_bias))
        prefix_kv = low(low_back(matmul(low(mid), kv_weight) + kv_bias))
        prefix_key = prefix_kv[:, :D]
        prefix_value = prefix_kv[:, D:]

        def step(carry, item):
            return (carry, jax.checkpoint(sequence_block)(item[0], item[1], prefix_key, prefix_value, frozen))
        _, outputs = lax.scan(step, jnp.zeros((), jnp.float32), (all_input.reshape(SEQUENCES, LENGTH, D), segment_rows))
        return outputs.reshape(SEQUENCES * LENGTH, D)
    primal = (tokens.astype(jnp.float32), prefix_embed.astype(jnp.float32), w_mid.astype(jnp.float32), b_mid.astype(jnp.float32), w_kv.astype(jnp.float32), b_kv.astype(jnp.float32))
    result, pullback = jax.vjp(forward, *primal)
    grads = pullback(cotangent.astype(jnp.float32))
    return (result.astype(jnp.bfloat16), grads[0].astype(jnp.bfloat16), grads[1], grads[2], grads[3], grads[4], grads[5])
```

```python
import jax
import jax.numpy as jnp
from jax import lax
from jax.experimental import pallas as pl
from jax.experimental.pallas import tpu as pltpu
from jax.sharding import PartitionSpec as P

HEAD=64; PREFIX=10; LENGTH=1024; PADP=16
LOG2E=1.4426950408889634
NEG=-1e30
KX=1152
NT=(((1,),(1,)),((),()))
NN=(((1,),(0,)),((),()))
TN=(((0,),(0,)),((),()))
def dg(a,b,d): return lax.dot_general(a,b,d,preferred_element_type=jnp.float32)
SCALE=HEAD**-0.5
C=SCALE*LOG2E

def split3(x):
    hi=x.astype(jnp.bfloat16); r=x-hi.astype(jnp.float32)
    mid=r.astype(jnp.bfloat16); r=r-mid.astype(jnp.float32)
    return hi.astype(jnp.float32),mid.astype(jnp.float32),r

QB=((0,240,256),(240,496,512),(496,752,768),(752,1024,1152))
def fwd_kernel(sc_ref, sr_ref, q_ref, k_ref, v_ref, pk_ref, pv_ref, o_ref, l_ref, bias, kx, vx):
    @pl.when(pl.program_id(0)==0)
    def _():
        row=lax.broadcasted_iota(jnp.int32,(LENGTH,KX),0)+PADP
        col=lax.broadcasted_iota(jnp.int32,(LENGTH,KX),1)
        ok=((sc_ref[...]==sr_ref[...])&(col<=row))|(col<PREFIX)
        bias[...]=jnp.where(ok,0.0,NEG)
        kx[...]=jnp.zeros_like(kx); vx[...]=jnp.zeros_like(vx)
    lane=lax.broadcasted_iota(jnp.int32,(1,128),1)
    for h in range(2):
        mh=((lane>=64*h)&(lane<64*h+64))
        z=jnp.bfloat16(0)
        kx[h,:PADP,:]=jnp.where(mh,pk_ref[...],z); kx[h,PADP:PADP+LENGTH,:]=jnp.where(mh,k_ref[...],z)
        vx[h,:PADP,:128]=jnp.where(mh,pv_ref[...],z); vx[h,PADP:PADP+LENGTH,:128]=jnp.where(mh,v_ref[...],z)
        vx[h,:,128:]=jnp.ones((KX,128),jnp.bfloat16)
    for a,b,nk in QB:
        outs=[]; ls=[]
        for h in range(2):
            s=dg(q_ref[a:b,:],kx[h,:nk,:],NT)
            s=s*C+bias[a:b,:nk]
            m=jnp.max(s,axis=1,keepdims=True)
            p=jnp.exp2(s-m).astype(jnp.bfloat16)
            o=dg(p,vx[h,:nk,:],NN)
            l=o[:,128:]
            outs.append(o[:,:128]/l)
            ls.append(-(m+jnp.log2(l))*(1.0/C))
        o_ref[a:b,:]=(outs[0]+outs[1]).astype(jnp.bfloat16)
        h0,m0,l0=split3(ls[0]); h1,m1,l1=split3(ls[1])
        aug=jnp.where(lane==0,h0,jnp.where(lane==1,m0,jnp.where(lane==2,l0,jnp.where(lane==3,h1,jnp.where(lane==4,m1,jnp.where(lane==5,l1,0.0))))))
        l_ref[a:b,:]=aug.astype(jnp.bfloat16)

def attn_fwd(qkv, prefix_kv16, seg):
    D=qkv.shape[1]//3; nh=D//128
    sc=seg[:,None]
    sr=jnp.concatenate([jnp.full((PADP,),-1,jnp.int32),seg,jnp.full((KX-PADP-LENGTH,),-1,jnp.int32)])[None,:]
    return pl.pallas_call(fwd_kernel,grid=(nh,),
      in_specs=[pl.BlockSpec((LENGTH,1),lambda h:(0,0)),pl.BlockSpec((1,KX),lambda h:(0,0)),
        pl.BlockSpec((LENGTH,128),lambda h:(0,h)),pl.BlockSpec((LENGTH,128),lambda h:(0,nh+h)),pl.BlockSpec((LENGTH,128),lambda h:(0,2*nh+h)),
        pl.BlockSpec((PADP,128),lambda h:(0,h)),pl.BlockSpec((PADP,128),lambda h:(0,nh+h))],
      out_specs=[pl.BlockSpec((LENGTH,128),lambda h:(0,h)),pl.BlockSpec((LENGTH,128),lambda h:(0,h))],
      out_shape=[jax.ShapeDtypeStruct((LENGTH,D),jnp.bfloat16),jax.ShapeDtypeStruct((LENGTH,D),jnp.bfloat16)],
      scratch_shapes=[pltpu.VMEM((LENGTH,KX),jnp.float32),pltpu.VMEM((2,KX,128),jnp.bfloat16),pltpu.VMEM((2,KX,256),jnp.bfloat16)],
      compiler_params=pltpu.CompilerParams(vmem_limit_bytes=48*1024*1024),
      cost_estimate=pl.CostEstimate(flops=4*1024*1024*1024,bytes_accessed=10*1024*1024,transcendentals=10*1024*1024),
    )(sc,sr,qkv,qkv,qkv,prefix_kv16,prefix_kv16)

KB=((0,272,0),(272,528,256),(528,784,512),(784,1040,768))
KY=1040
def make_bwd(variant):
  def bwd_kernel(sc_ref, sr_ref, q_ref, k_ref, v_ref, pk_ref, pv_ref, l_ref, o_ref, g_ref,
                 dq_ref, dk_ref, dv_ref, dpk_ref, dpv_ref, bias, qa, ga, ka, va, dq):
    @pl.when(pl.program_id(0)==0)
    def _():
        row=lax.broadcasted_iota(jnp.int32,(KY,LENGTH),0)
        col=lax.broadcasted_iota(jnp.int32,(KY,LENGTH),1)+PADP
        ok=((sc_ref[...]==sr_ref[...])&(row<=col))|(row<PREFIX)
        bias[...]=jnp.where(ok,0.0,NEG)
    lane=lax.broadcasted_iota(jnp.int32,(1,128),1)
    z=jnp.bfloat16(0)
    qa[:,:128]=q_ref[...]; qa[:,128:]=l_ref[...]
    ga[:,:128]=g_ref[...]
    prod=g_ref[...].astype(jnp.float32)*o_ref[...].astype(jnp.float32)
    aug=None
    for h in range(2):
        mh=((lane>=64*h)&(lane<64*h+64))
        d=-jnp.sum(jnp.where(mh,prod,0.0),axis=1,keepdims=True)
        hi,mid,lo=split3(d)
        t=jnp.where(lane==3*h,hi,jnp.where(lane==3*h+1,mid,jnp.where(lane==3*h+2,lo,0.0)))
        aug=t if aug is None else aug+t
        one=jnp.where((lane>=3*h)&(lane<3*h+3),1.0,0.0).astype(jnp.bfloat16)
        ka[h,:PADP,:128]=jnp.where(mh,pk_ref[...],z); ka[h,PADP:,:128]=jnp.where(mh,k_ref[...],z)
        va[h,:PADP,:128]=jnp.where(mh,pv_ref[...],z); va[h,PADP:,:128]=jnp.where(mh,v_ref[...],z)
        ka[h,:,128:]=jnp.broadcast_to(one,(KY,128)); va[h,:,128:]=jnp.broadcast_to(one,(KY,128))
    ga[:,128:]=aug.astype(jnp.bfloat16)
    for i,(a,b,q0) in enumerate(KB):
        dk=None; dv=None; dqs=[]
        for h in range(2):
            mh=((lane>=64*h)&(lane<64*h+64))
            s=dg(ka[h,a:b,:],qa[q0:,:],NT)
            p=jnp.exp2(s*C+bias[a:b,q0:])
            dp=dg(va[h,a:b,:],ga[q0:,:],NT)
            ds=(p*dp).astype(jnp.bfloat16)
            pb=p.astype(jnp.bfloat16)
            tv=dg(pb,jnp.where(mh,g_ref[q0:,:],z),NN)
            tk=dg(ds,jnp.where(mh,q_ref[q0:,:],z),NN)
            dv=tv if dv is None else dv+tv
            dk=tk if dk is None else dk+tk
            if variant=="tn":
                dqs.append(dg(ds,ka[h,a:b,:128],TN))
            else:
                kt=ka[h,a:b,:128].T
                dqs.append(dg(kt,ds,NN))
        t=dqs[0]+dqs[1]
        if variant=="tn":
            if i==0: dq[...]=t
            else: dq[q0:,:]+=t
        else:
            if i==0: dq[...]=t
            else: dq[:,q0:]+=t
        if i==0:
            dpk_ref[...]=dk[:PADP]*SCALE; dpv_ref[...]=dv[:PADP]
            dk_ref[:256,:]=(dk[PADP:]*SCALE).astype(jnp.bfloat16); dv_ref[:256,:]=dv[PADP:].astype(jnp.bfloat16)
        else:
            dk_ref[q0:q0+256,:]=(dk*SCALE).astype(jnp.bfloat16); dv_ref[q0:q0+256,:]=dv.astype(jnp.bfloat16)
    r=dq[...] if variant=="tn" else dq[...].T
    dq_ref[...]=(r*SCALE).astype(jnp.bfloat16)
  return bwd_kernel

def attn_bwd(qkv, prefix_kv16, seg, lse, o, g, variant="tn"):
    D=qkv.shape[1]//3; nh=D//128
    sr=seg[None,:]
    sc=jnp.concatenate([jnp.full((PADP,),-1,jnp.int32),seg])[:,None]
    blk=lambda off: pl.BlockSpec((LENGTH,128),lambda h,off=off:(0,off+h))
    pblk=lambda off: pl.BlockSpec((PADP,128),lambda h,off=off:(0,off+h))
    return pl.pallas_call(make_bwd(variant),grid=(nh,),
      in_specs=[pl.BlockSpec((KY,1),lambda h:(0,0)),pl.BlockSpec((1,LENGTH),lambda h:(0,0)),
        blk(0),blk(nh),blk(2*nh),pblk(0),pblk(nh),blk(0),blk(0),blk(0)],
      out_specs=[blk(0)]*3+[pblk(0)]*2,
      out_shape=[jax.ShapeDtypeStruct((LENGTH,D),jnp.bfloat16)]*3+[jax.ShapeDtypeStruct((PADP,D),jnp.float32)]*2,
      scratch_shapes=[pltpu.VMEM((KY,LENGTH),jnp.float32),pltpu.VMEM((LENGTH,256),jnp.bfloat16),pltpu.VMEM((LENGTH,256),jnp.bfloat16),
         pltpu.VMEM((2,KY,256),jnp.bfloat16),pltpu.VMEM((2,KY,256),jnp.bfloat16),
         pltpu.VMEM((LENGTH,128) if variant=="tn" else (128,LENGTH),jnp.float32)],
      compiler_params=pltpu.CompilerParams(vmem_limit_bytes=56*1024*1024),
      cost_estimate=pl.CostEstimate(flops=10*1024*1024*1024,bytes_accessed=16*1024*1024,transcendentals=10*1024*1024),
    )(sc,sr,qkv,qkv,qkv,prefix_kv16,prefix_kv16,lse,o,g)


def layer_norm(values, gain_row, shift_row):
    row_mean = jnp.mean(values, axis=-1, keepdims=True)
    centred = values - row_mean
    spread = jnp.mean(centred * centred, axis=-1, keepdims=True)
    return centred * lax.rsqrt(spread + 1e-05) * gain_row + shift_row


def norm_back(values, gain_row, grad_in):

    def apply_norm(inner_values):
        return layer_norm(inner_values, gain_row, 0.0)

    _, pullback = jax.vjp(apply_norm, values)
    return pullback(grad_in)[0]


def gelu_tanh(values):
    return jax.nn.gelu(values, approximate=True)


def dot_plain(left, right):
    return jnp.dot(left, right, preferred_element_type=jnp.float32)


def dot_first(left, right):
    return lax.dot_general(
        left, right, (((0,), (0,)), ((), ())), preferred_element_type=jnp.float32
    )


def dot_second(left, right):
    return lax.dot_general(
        left, right, (((1,), (1,)), ((), ())), preferred_element_type=jnp.float32
    )


def adapter_back(prefix_low, prefix_embed, w_mid, w_kv, mid_act):
    grad_kv_w = dot_first(mid_act.astype(jnp.bfloat16), prefix_low)
    grad_kv_b = jnp.sum(prefix_low.astype(jnp.float32), axis=0)
    grad_mid = dot_second(prefix_low, w_kv)
    grad_mid_low = (grad_mid * (1.0 - mid_act * mid_act)).astype(jnp.bfloat16)
    grad_mid_w = dot_first(prefix_embed, grad_mid_low)
    grad_mid_b = jnp.sum(grad_mid_low.astype(jnp.float32), axis=0)
    grad_embed = dot_second(grad_mid_low, w_mid)
    return (grad_embed, grad_mid_w, grad_mid_b, grad_kv_w, grad_kv_b)


def body(
    tokens,
    segments,
    cotangent,
    ln1_gain,
    ln1_bias,
    w_qkv,
    b_qkv,
    w_out,
    b_out,
    ln2_gain,
    ln2_bias,
    w_fc,
    b_fc,
    w_proj,
    b_proj,
    prefix_embed,
    w_mid,
    b_mid,
    w_kv,
    b_kv,
):
    gain_one, shift_one, qkv_weight, qkv_bias, out_weight, out_bias = (
        lax.all_gather(ln1_gain, ("dp", "fsdp"), axis=0, tiled=True),
        lax.all_gather(ln1_bias, ("dp", "fsdp"), axis=0, tiled=True),
        lax.all_gather(w_qkv, ("dp", "fsdp"), axis=0, tiled=True),
        lax.all_gather(b_qkv, ("dp", "fsdp"), axis=0, tiled=True),
        lax.all_gather(w_out, ("dp", "fsdp"), axis=0, tiled=True),
        lax.all_gather(b_out, ("dp", "fsdp"), axis=0, tiled=True),
    )
    gain_two, shift_two, fc_weight, fc_bias, proj_weight, proj_bias = (
        lax.all_gather(ln2_gain, ("dp", "fsdp"), axis=0, tiled=True),
        lax.all_gather(ln2_bias, ("dp", "fsdp"), axis=0, tiled=True),
        lax.all_gather(w_fc, ("dp", "fsdp"), axis=0, tiled=True),
        lax.all_gather(b_fc, ("dp", "fsdp"), axis=0, tiled=True),
        lax.all_gather(w_proj, ("dp", "fsdp"), axis=0, tiled=True),
        lax.all_gather(b_proj, ("dp", "fsdp"), axis=0, tiled=True),
    )
    mid_act = jnp.tanh(dot_plain(prefix_embed, w_mid) + b_mid.astype(jnp.float32))
    prefix_kv = (dot_plain(mid_act.astype(jnp.bfloat16), w_kv) + b_kv.astype(jnp.float32)).astype(
        jnp.bfloat16
    )
    prefix_pad = jnp.pad(prefix_kv, ((0, PADP - PREFIX), (0, 0)))
    residual_in = tokens.astype(jnp.float32)
    normed_one = layer_norm(
        residual_in, gain_one.astype(jnp.float32), shift_one.astype(jnp.float32)
    )
    qkv_low = (
        dot_plain(normed_one.astype(jnp.bfloat16), qkv_weight) + qkv_bias.astype(jnp.float32)
    ).astype(jnp.bfloat16)
    hidden_low, lse_aug = attn_fwd(qkv_low, prefix_pad, segments)
    mixed = residual_in + dot_plain(hidden_low, out_weight) + out_bias.astype(jnp.float32)
    normed_two = layer_norm(mixed, gain_two.astype(jnp.float32), shift_two.astype(jnp.float32))
    pre_act = dot_plain(normed_two.astype(jnp.bfloat16), fc_weight) + fc_bias.astype(jnp.float32)
    act_low = gelu_tanh(pre_act).astype(jnp.bfloat16)
    block_out = (mixed + dot_plain(act_low, proj_weight) + proj_bias.astype(jnp.float32)).astype(
        jnp.bfloat16
    )
    gain_two_back, fc_back, proj_back = (
        lax.all_gather(ln2_gain, ("dp", "fsdp"), axis=0, tiled=True),
        lax.all_gather(w_fc, ("dp", "fsdp"), axis=0, tiled=True),
        lax.all_gather(w_proj, ("dp", "fsdp"), axis=0, tiled=True),
    )
    grad_act = dot_second(cotangent, proj_back)
    _, gelu_pull = jax.vjp(gelu_tanh, pre_act)
    grad_pre = gelu_pull(grad_act)[0].astype(jnp.bfloat16)
    grad_normed_two = dot_second(grad_pre, fc_back)
    grad_mixed = cotangent.astype(jnp.float32) + norm_back(
        mixed, gain_two_back.astype(jnp.float32), grad_normed_two
    )
    gain_one_back, qkv_back, out_back = (
        lax.all_gather(ln1_gain, ("dp", "fsdp"), axis=0, tiled=True),
        lax.all_gather(w_qkv, ("dp", "fsdp"), axis=0, tiled=True),
        lax.all_gather(w_out, ("dp", "fsdp"), axis=0, tiled=True),
    )
    grad_hidden = dot_second(grad_mixed.astype(jnp.bfloat16), out_back).astype(jnp.bfloat16)
    gq, gk, gv, gpk, gpv = attn_bwd(qkv_low, prefix_pad, segments, lse_aug, hidden_low, grad_hidden, "kt")
    grad_qkv = jnp.concatenate([gq, gk, gv], 1)
    grad_prefix = jnp.concatenate([gpk[:PREFIX], gpv[:PREFIX]], 1)
    total_prefix = lax.psum(grad_prefix, ("dp", "fsdp"))
    grad_embed, grad_mid_w, grad_mid_b, grad_kv_w, grad_kv_b = adapter_back(
        total_prefix.astype(jnp.bfloat16), prefix_embed, w_mid, w_kv, mid_act
    )
    grad_normed_one = dot_second(grad_qkv, qkv_back)
    grad_tokens = (
        grad_mixed + norm_back(residual_in, gain_one_back.astype(jnp.float32), grad_normed_one)
    ).astype(jnp.bfloat16)
    return (block_out, grad_tokens, grad_embed, grad_mid_w, grad_mid_b, grad_kv_w, grad_kv_b)


def solution(mesh):
    return jax.shard_map(
        body,
        mesh=mesh,
        in_specs=(
            P(("dp", "fsdp"), None),
            P(("dp", "fsdp")),
            P(("dp", "fsdp"), None),
            P(("dp", "fsdp")),
            P(("dp", "fsdp")),
            P(("dp", "fsdp"), None),
            P(("dp", "fsdp")),
            P(("dp", "fsdp"), None),
            P(("dp", "fsdp")),
            P(("dp", "fsdp")),
            P(("dp", "fsdp")),
            P(("dp", "fsdp"), None),
            P(("dp", "fsdp")),
            P(("dp", "fsdp"), None),
            P(("dp", "fsdp")),
            P(),
            P(),
            P(),
            P(),
            P(),
        ),
        out_specs=(P(("dp", "fsdp"), None), P(("dp", "fsdp"), None), P(), P(), P(), P(), P()),
        check_vma=False,
    )
```

```python
import jax
import jax.numpy as jnp
from jax import lax
from jax.experimental import pallas as pl
from jax.experimental.pallas import tpu as pltpu
from jax.sharding import PartitionSpec as P

HEAD = 64
PREFIX = 10
PADP = 16
LENGTH = 1024
AXES = ("dp", "fsdp")
LOG2E = 1.4426950408889634
SCALE = HEAD**-0.5
C2 = SCALE * LOG2E
NEG = -1e30
KX = 1152
KY = PADP + LENGTH
NT = (((1,), (1,)), ((), ()))
NN = (((1,), (0,)), ((), ()))
TN = (((0,), (0,)), ((), ()))
PIECES = 32
MB = 1024 * 1024


def dg(left, right, dims):
    return lax.dot_general(left, right, dims, preferred_element_type=jnp.float32)


def f32(value):
    return value.astype(jnp.float32)


def low(value):
    return value.astype(jnp.bfloat16)


def params():
    return pltpu.CompilerParams(vmem_limit_bytes=60 * MB)


def flip_dp(value, mask, size):
    return lax.ppermute(value, "dp", [(i, i ^ mask) for i in range(size)])


def flip_z(value, mask, size):
    return lax.ppermute(value, "fsdp", [(i, i ^ mask) for i in range(size)])


def fence(*values):
    return lax.optimization_barrier(values)


def z_stage(shard, fsdp):
    own = shard[None]
    return [own] + [flip_z(own, m, fsdp) for m in (2, 1, 3)]


def first_stage(near, far, dp):
    return near, far, flip_dp(near, 2, dp), flip_dp(far, 4, dp)


def glue_kernel(a_ref, b_ref, c_ref, d_ref, near_ref, far_ref):
    size = a_ref.shape[0]
    near_ref[:size] = a_ref[...]
    near_ref[size:] = b_ref[...]
    far_ref[:size] = c_ref[...]
    far_ref[size:] = d_ref[...]


def glue(a, b, c, d):
    vmem = pl.BlockSpec(memory_space=pltpu.VMEM)
    shape = (2 * a.shape[0],) + a.shape[1:]
    return pl.pallas_call(
        glue_kernel,
        in_specs=[vmem] * 4,
        out_specs=[vmem] * 2,
        out_shape=[jax.ShapeDtypeStruct(shape, a.dtype)] * 2,
    )(a, b, c, d)


def join_stage(state):
    return glue(state[0], state[2], state[1], state[3])


def second_stage(near, far, dp):
    return [near, flip_dp(near, 4, dp), far, flip_dp(far, 2, dp)]


def core_stage(plane, dp):
    return plane + [flip_dp(one, 1, dp) for one in plane]


def place_order(dp, fsdp):
    d = lax.axis_index("dp")
    z = lax.axis_index("fsdp")
    places = []
    for core in (0, 1):
        for first, second, base in ((2, 4, 0), (4, 2, 1)):
            for outer in (0, second):
                for inner in (0, first):
                    for turn in (base, base ^ 2):
                        places.append((d ^ (core ^ outer ^ inner)) * fsdp + (z ^ turn))
    return jnp.stack(places).astype(jnp.int32)


SMALL = 8


def pack_kernel(*refs):
    ins, out_ref = refs[:SMALL], refs[SMALL]
    row = jnp.zeros((SMALL, 128), jnp.float32)
    spot = lax.broadcasted_iota(jnp.int32, (SMALL, 128), 0)
    for i, one in enumerate(ins):
        wide = one.shape[1]
        value = f32(one[...])
        if wide < 128:
            value = jnp.concatenate([value, jnp.zeros((1, 128 - wide), jnp.float32)], 1)
        row = jnp.where(spot == i, value, row)
    out_ref[...] = jnp.broadcast_to(low(row)[None], out_ref.shape)


def pack_call(small, devices):
    vmem = pl.BlockSpec(memory_space=pltpu.VMEM)
    return pl.pallas_call(
        pack_kernel,
        in_specs=[vmem] * SMALL,
        out_specs=vmem,
        out_shape=jax.ShapeDtypeStruct((devices, SMALL, 128), jnp.bfloat16),
    )(*[one[None] for one in small])


def unpack_kernel(widths, all_ref, rows_ref, qa_ref, qb_ref, fc_ref):
    devices = all_ref.shape[0]
    depth = rows_ref.shape[1]
    half = depth // 2

    def spread(i, place):
        share = all_ref[:, i, :]
        lane = lax.broadcasted_iota(jnp.int32, (128, place.shape[1]), 0)
        pick = low(jnp.where(lane == place % widths[i], 1.0, 0.0))
        owner = lax.broadcasted_iota(jnp.int32, (devices, place.shape[1]), 0)
        found = jnp.where(owner == place // widths[i], dg(share, pick, NN), 0.0)
        return jnp.sum(found, axis=0, keepdims=True)

    natural = lax.broadcasted_iota(jnp.int32, (1, depth), 1)
    for i in range(SMALL - 2):
        rows_ref[i : i + 1, :] = spread(i, natural)
    rows_ref[SMALL - 2 :, :] = jnp.zeros((2, depth), jnp.float32)
    short = lax.broadcasted_iota(jnp.int32, (1, half), 1)
    for k in range(3):
        qa_ref[:, k * half : (k + 1) * half] = spread(SMALL - 2, short + k * depth)
        qb_ref[:, k * half : (k + 1) * half] = spread(SMALL - 2, short + k * depth + half)
    for k in range(fc_ref.shape[1] // depth):
        fc_ref[:, k * depth : (k + 1) * depth] = spread(SMALL - 1, natural + k * depth)


def unpack_call(gathered, widths, depth, wide):
    vmem = pl.BlockSpec(memory_space=pltpu.VMEM)
    shapes = ((SMALL, depth), (1, 3 * depth // 2), (1, 3 * depth // 2), (1, wide))
    return pl.pallas_call(
        lambda *refs: unpack_kernel(widths, *refs),
        in_specs=[vmem],
        out_specs=[vmem] * 4,
        out_shape=[jax.ShapeDtypeStruct(shape, jnp.float32) for shape in shapes],
    )(gathered)


def adapter_kernel(embed_ref, wm_ref, bm_ref, wkv_ref, bkv_ref, mid_ref, kv_ref):
    mid = jnp.tanh(dg(embed_ref[...], wm_ref[...], NN) + f32(bm_ref[...]))
    mid_ref[...] = mid
    kv = low(dg(low(mid), wkv_ref[...], NN) + f32(bkv_ref[...]))
    row = lax.broadcasted_iota(jnp.int32, kv.shape, 0)
    kv_ref[...] = jnp.where(row < PREFIX, kv, jnp.bfloat16(0))


def adapter_call(embed, w_mid, b_mid, w_kv, b_kv):
    vmem = pl.BlockSpec(memory_space=pltpu.VMEM)
    return pl.pallas_call(
        adapter_kernel,
        in_specs=[vmem] * 5,
        out_specs=[vmem] * 2,
        out_shape=[
            jax.ShapeDtypeStruct((PADP, w_mid.shape[1]), jnp.float32),
            jax.ShapeDtypeStruct((PADP, w_kv.shape[1]), jnp.bfloat16),
        ],
    )(embed, w_mid, b_mid[None], w_kv, b_kv[None])


def adapter_back_kernel(
    own_ref, other_ref, embed_ref, wm_ref, wkv_ref, mid_ref, ge_ref, gmw_ref, gmb_ref, gkw_ref, gkb_ref
):
    low_sum = low(own_ref[...] + other_ref[...])
    mid = mid_ref[...]
    gkw_ref[...] = dg(low(mid), low_sum, TN)
    gkb_ref[...] = jnp.sum(f32(low_sum), axis=0, keepdims=True)
    grad = low(dg(low_sum, wkv_ref[...], NT) * (1.0 - mid * mid))
    gmw_ref[...] = dg(embed_ref[...], grad, TN)
    gmb_ref[...] = jnp.sum(f32(grad), axis=0, keepdims=True)
    ge_ref[...] = dg(grad, wm_ref[...], NT)[:PREFIX]


def adapter_back_call(own, other, embed, w_mid, w_kv, mid):
    vmem = pl.BlockSpec(memory_space=pltpu.VMEM)
    depth, middle = w_mid.shape
    shapes = ((PREFIX, depth), (depth, middle), (1, middle), w_kv.shape, (1, w_kv.shape[1]))
    found = pl.pallas_call(
        adapter_back_kernel,
        in_specs=[vmem] * 6,
        out_specs=[vmem] * 5,
        out_shape=[jax.ShapeDtypeStruct(shape, jnp.float32) for shape in shapes],
    )(own, other, embed, w_mid, w_kv, mid)
    return found[0], found[1], found[2][0], found[3], found[4][0]


def gather_small(small, devices):
    return lax.all_to_all(pack_call(small, devices), AXES, 0, 0, tiled=True)


def natural_pieces(shard):
    whole = lax.all_gather(shard, AXES, axis=0, tiled=True)
    whole = whole.reshape(8, 4, whole.shape[0] // PIECES, *whole.shape[1:])
    return [whole[i] for i in range(8)]


def place_pieces(order_ref, piece_refs, target_ref, columns, sems):
    copies = []
    for b in range(8):
        for k in range(4):
            i = b * 4 + k
            row = pl.multiple_of(order_ref[i] * PIECES, PIECES)
            copies.append(
                pltpu.make_async_copy(
                    piece_refs[b].at[k, :, columns],
                    target_ref.at[pl.ds(row, PIECES), :],
                    sems.at[i],
                )
            )
    return copies


def anyspec():
    return pl.BlockSpec(memory_space=pl.ANY)


def smem():
    return pl.BlockSpec(memory_space=pltpu.SMEM)


def norm_rows(values):
    mean = jnp.mean(values, axis=-1, keepdims=True)
    centred = values - mean
    spread = jnp.mean(centred * centred, axis=-1, keepdims=True)
    return centred * lax.rsqrt(spread + 1e-05), spread


def norm_pull(values, gain_row, grad):
    unit, spread = norm_rows(values)
    weighted = grad * gain_row
    first = jnp.mean(weighted, axis=-1, keepdims=True)
    second = jnp.mean(weighted * unit, axis=-1, keepdims=True)
    return (weighted - first - unit * second) * lax.rsqrt(spread + 1e-05)


def out_kernel(column, order_ref, tokens_ref, ha_ref, hb_ref, vec_ref, *rest):
    pieces, (mixed_ref, normed_ref, weight_ref, sems) = rest[:8], rest[8:]

    @pl.when(pl.program_id(0) == 0)
    def _():
        width = weight_ref.shape[1]
        copies = place_pieces(order_ref, pieces, weight_ref, pl.ds(column, width), sems)
        for one in copies:
            one.start()
        for one in copies:
            one.wait()

    half = ha_ref.shape[1]
    mixed = f32(tokens_ref[...]) + vec_ref[2:3, :]
    mixed += dg(ha_ref[...], weight_ref[:half, :], NN)
    mixed += dg(hb_ref[...], weight_ref[half:, :], NN)
    mixed_ref[...] = mixed
    unit, _ = norm_rows(mixed)
    normed_ref[...] = low(unit * vec_ref[3:4, :] + vec_ref[4:5, :])


def out_call(order, tokens, hidden_a, hidden_b, vectors, pieces, column, block=256):
    rows, depth = tokens.shape
    row = lambda w: pl.BlockSpec((block, w), lambda i: (i, 0))
    whole = lambda s: pl.BlockSpec(s, lambda i: (0, 0))
    return pl.pallas_call(
        lambda *refs: out_kernel(column, *refs),
        grid=(rows // block,),
        in_specs=[smem(), row(depth), row(depth // 2), row(depth // 2), whole(vectors.shape)]
        + [anyspec()] * 8,
        out_specs=[row(depth), row(depth), whole((depth, depth))],
        out_shape=[
            jax.ShapeDtypeStruct((rows, depth), jnp.float32),
            jax.ShapeDtypeStruct((rows, depth), jnp.bfloat16),
            jax.ShapeDtypeStruct((depth, depth), jnp.bfloat16),
        ],
        scratch_shapes=[pltpu.SemaphoreType.DMA((PIECES,))],
        compiler_params=params(),
    )(order, tokens, hidden_a, hidden_b, vectors, *pieces)


GELU_A = 0.7978845608028654
GELU_B = 0.044715


def gelu_pair(value):
    square = value * value
    half = 0.5 + 0.5 * jnp.tanh(value * (GELU_A + GELU_A * GELU_B * square))
    act = value * half
    slope = half + 2.0 * act * (1.0 - half) * (GELU_A + 3.0 * GELU_A * GELU_B * square)
    return act, slope


def gact_kernel(cot_ref, proj_ref, out_ref):
    out_ref[...] = low(dg(cot_ref[...], proj_ref[...], NT))


def gact_call(cot, proj, block=1024):
    rows, depth = cot.shape
    wide = proj.shape[0]
    return pl.pallas_call(
        gact_kernel,
        grid=(wide // block,),
        in_specs=[
            pl.BlockSpec((rows, depth), lambda j: (0, 0)),
            pl.BlockSpec((block, depth), lambda j: (j, 0)),
        ],
        out_specs=pl.BlockSpec((rows, block), lambda j: (0, j)),
        out_shape=jax.ShapeDtypeStruct((rows, wide), jnp.bfloat16),
        compiler_params=params(),
    )(cot, proj)


def ffn_kernel(
    order_ref, normed_ref, cot_ref, gact_ref, bias_ref, mixed_ref, vec_ref, wout_ref, all_ref, *rest
):
    pieces = rest[:8]
    block_ref, gmix_ref, ghid_ref, fc_ref, proj_ref, acc_ref, gacc_ref, sems, psems = rest[8:]
    i = pl.program_id(0)
    blocks, depth = fc_ref.shape[0], normed_ref.shape[1]

    def copies(k):
        found = []
        for p in range(PIECES):
            row = pl.multiple_of(order_ref[p] * PIECES, PIECES)
            source = pieces[p // 4].at[p % 4, :, pl.ds(k * depth, depth)]
            target = fc_ref.at[k, pl.ds(row, PIECES), :]
            found.append(pltpu.make_async_copy(source, target, sems.at[k, p]))
        source = all_ref.at[pl.ds(k * depth, depth), :]
        return found + [pltpu.make_async_copy(source, proj_ref.at[k], psems.at[k])]

    @pl.when(i == 0)
    def _():
        for k in range(blocks):
            for one in copies(k):
                one.start()

    for k in range(blocks):

        @pl.when(i == 0)
        def _(k=k):
            for one in copies(k):
                one.wait()

        c = slice(k * depth, (k + 1) * depth)
        pre = dg(normed_ref[...], fc_ref[k], NN) + bias_ref[:, c]
        act, slope = gelu_pair(pre)
        gpre = low(f32(gact_ref[:, c]) * slope)
        out = dg(low(act), proj_ref[k], NN)
        gnorm = dg(gpre, fc_ref[k], NT)
        if k == 0:
            acc_ref[...] = out
            gacc_ref[...] = gnorm
        else:
            acc_ref[...] += out
            gacc_ref[...] += gnorm

    mixed = mixed_ref[...]
    block_ref[...] = low(mixed + acc_ref[...] + vec_ref[5:6, :])
    gmix = f32(cot_ref[...]) + norm_pull(mixed, vec_ref[3:4, :], gacc_ref[...])
    gmix_ref[...] = gmix
    ghid_ref[...] = low(dg(low(gmix), wout_ref[...], NT))


def ffn_call(order, normed, cot, gact, bias, mixed, vectors, wout, proj, pieces, block=512):
    rows, depth = normed.shape
    wide = gact.shape[1]
    blocks = wide // depth
    row = pl.BlockSpec((block, depth), lambda i: (i, 0))
    whole = lambda a: pl.BlockSpec(a.shape, lambda i: (0, 0))
    return pl.pallas_call(
        ffn_kernel,
        grid=(rows // block,),
        in_specs=[smem(), row, row, pl.BlockSpec((block, wide), lambda i: (i, 0)), whole(bias)]
        + [row, whole(vectors), whole(wout), anyspec()]
        + [anyspec()] * 8,
        out_specs=[row] * 3,
        out_shape=[
            jax.ShapeDtypeStruct((rows, depth), jnp.bfloat16),
            jax.ShapeDtypeStruct((rows, depth), jnp.float32),
            jax.ShapeDtypeStruct((rows, depth), jnp.bfloat16),
        ],
        scratch_shapes=[pltpu.VMEM((blocks, depth, depth), jnp.bfloat16)] * 2
        + [pltpu.VMEM((block, depth), jnp.float32)] * 2
        + [pltpu.SemaphoreType.DMA((blocks, PIECES)), pltpu.SemaphoreType.DMA((blocks,))],
        compiler_params=params(),
    )(order, normed, cot, gact, bias, mixed, vectors, wout, proj, *pieces)


def final_kernel(tokens_ref, gmix_ref, vec_ref, wa_ref, wb_ref, *rest):
    grads, out_ref = rest[:6], rest[6]
    total = None
    for i in range(6):
        half = grads[i].shape[1]
        c = (i % 3) * half
        weight = (wa_ref if i < 3 else wb_ref)[:, c : c + half]
        part = dg(grads[i][...], weight, NT)
        total = part if total is None else total + part
    pulled = norm_pull(f32(tokens_ref[...]), vec_ref[0:1, :], total)
    out_ref[...] = low(gmix_ref[...] + pulled)


def final_call(tokens, gmix, vectors, wa, wb, grads, block=256):
    rows, depth = tokens.shape
    row = lambda w: pl.BlockSpec((block, w), lambda i: (i, 0))
    whole = lambda s: pl.BlockSpec(s, lambda i: (0, 0))
    return pl.pallas_call(
        final_kernel,
        grid=(rows // block,),
        in_specs=[row(depth), row(depth), whole(vectors.shape), whole(wa.shape), whole(wb.shape)]
        + [row(grads[0].shape[1])] * 6,
        out_specs=row(depth),
        out_shape=jax.ShapeDtypeStruct((rows, depth), jnp.bfloat16),
        compiler_params=params(),
    )(tokens, gmix, vectors, wa, wb, *grads)


def split3(value):
    high = f32(low(value))
    rest = value - high
    middle = f32(low(rest))
    return high, middle, rest - middle


QUERY_BLOCKS = ((0, 240, 256), (240, 496, 512), (496, 752, 768), (752, 1024, 1152))
KEY_BLOCKS = ((0, 272, 0), (272, 528, 256), (528, 784, 512), (784, 1040, 768))


def as_column(row):
    return jnp.broadcast_to(f32(row), (8, row.shape[1])).T[:, 0:1].astype(jnp.int32)


def head_lanes(h):
    lane = lax.broadcasted_iota(jnp.int32, (1, 128), 1)
    return (lane >= HEAD * h) & (lane < HEAD * h + HEAD)


def front_kernel(
    order_ref, seg_ref, keys_ref, tokens_ref, vec_ref, qb_ref, pk_ref, pv_ref, *rest
):
    pieces, (o_ref, l_ref, qkv_ref, weight_ref, bias, kx, vx, normed, sems) = rest[:8], rest[8:]
    step = pl.program_id(0)
    width = weight_ref.shape[1]

    @pl.when(step == 0)
    def _():
        copies = place_pieces(order_ref, pieces, weight_ref, pl.ds(0, width), sems)
        for one in copies:
            one.start()
        row = lax.broadcasted_iota(jnp.int32, (LENGTH, KX), 0) + PADP
        col = lax.broadcasted_iota(jnp.int32, (LENGTH, KX), 1)
        seen = ((as_column(seg_ref[...]) == keys_ref[...]) & (col <= row)) | (col < PREFIX)
        bias[...] = jnp.where(seen, 0.0, NEG)
        unit, _ = norm_rows(f32(tokens_ref[...]))
        normed[...] = low(unit * vec_ref[0:1, :] + vec_ref[1:2, :])
        kx[...] = jnp.zeros_like(kx)
        vx[...] = jnp.zeros_like(vx)
        for h in range(2):
            vx[h, :, 128:] = jnp.ones((KX, 128), jnp.bfloat16)
        for one in copies:
            one.wait()
        for c in range(0, width, 512):
            part = dg(normed[...], weight_ref[:, c : c + 512], NN) + qb_ref[:, c : c + 512]
            qkv_ref[:, c : c + 512] = low(part)

    lane = lax.broadcasted_iota(jnp.int32, (1, 128), 1)
    zero = jnp.bfloat16(0)
    at = [pl.ds(pl.multiple_of(i * (width // 3) + step * 128, 128), 128) for i in range(3)]
    for h in range(2):
        mine = head_lanes(h)
        kx[h, :PADP, :] = jnp.where(mine, pk_ref[...], zero)
        kx[h, PADP:KY, :] = jnp.where(mine, qkv_ref[:, at[1]], zero)
        vx[h, :PADP, :128] = jnp.where(mine, pv_ref[...], zero)
        vx[h, PADP:KY, :128] = jnp.where(mine, qkv_ref[:, at[2]], zero)
    for a, b, nk in QUERY_BLOCKS:
        outs, sums = [], []
        for h in range(2):
            s = dg(qkv_ref[a:b, at[0]], kx[h, :nk, :], NT) * C2 + bias[a:b, :nk]
            top = jnp.max(s, axis=1, keepdims=True)
            o = dg(low(jnp.exp2(s - top)), vx[h, :nk, :], NN)
            mass = o[:, 128:]
            outs.append(o[:, :128] / mass)
            sums.append((top + jnp.log2(mass)) * (-1.0 / C2))
        o_ref[a:b, :] = low(outs[0] + outs[1])
        aug = 0.0
        for i, part in enumerate(split3(sums[0]) + split3(sums[1])):
            aug = jnp.where(lane == i, part, aug)
        l_ref[a:b, :] = low(aug)


def segment_edges(segments):
    keys = jnp.pad(segments, (PADP, KX - KY), constant_values=-1)
    return segments[None, :], keys[None, :]


def front_call(order, edges, tokens, vectors, qkv_bias, prefix, first, pieces):
    depth = tokens.shape[1]
    width = qkv_bias.shape[1]
    pairs = width // 3 // 128
    whole = lambda s: pl.BlockSpec(s, lambda h: (0, 0), pipeline_mode=pl.Buffered(1))
    blk = pl.BlockSpec((LENGTH, 128), lambda h: (0, h))
    pblk = lambda off: pl.BlockSpec((PADP, 128), lambda h: (0, off + first + h))
    return pl.pallas_call(
        front_kernel,
        grid=(pairs,),
        in_specs=[smem(), whole((1, LENGTH)), whole((1, KX)), whole(tokens.shape)]
        + [whole(vectors.shape), whole(qkv_bias.shape), pblk(0), pblk(depth // 128)]
        + [anyspec()] * 8,
        out_specs=[blk, blk, whole((LENGTH, width)), whole((depth, width))],
        out_shape=[jax.ShapeDtypeStruct((LENGTH, width // 3), jnp.bfloat16)] * 2
        + [
            jax.ShapeDtypeStruct((LENGTH, width), jnp.bfloat16),
            jax.ShapeDtypeStruct((depth, width), jnp.bfloat16),
        ],
        scratch_shapes=[
            pltpu.VMEM((LENGTH, KX), jnp.float32),
            pltpu.VMEM((2, KX, 128), jnp.bfloat16),
            pltpu.VMEM((2, KX, 256), jnp.bfloat16),
            pltpu.VMEM(tokens.shape, jnp.bfloat16),
            pltpu.SemaphoreType.DMA((PIECES,)),
        ],
        compiler_params=params(),
    )(order, *edges, tokens, vectors, qkv_bias, prefix, prefix, *pieces)


def backward_kernel(
    seg_ref, keys_ref, q_ref, k_ref, v_ref, pk_ref, pv_ref, l_ref, o_ref, g_ref,
    dq_ref, dk_ref, dv_ref, bias, qa, ga, ka, va, dq,
):
    @pl.when(pl.program_id(0) == 0)
    def _():
        row = lax.broadcasted_iota(jnp.int32, (KY, LENGTH), 0)
        col = lax.broadcasted_iota(jnp.int32, (KY, LENGTH), 1) + PADP
        keys = as_column(keys_ref[...])[:KY]
        seen = ((keys == seg_ref[...]) & (row <= col)) | (row < PREFIX)
        bias[...] = jnp.where(seen, 0.0, NEG)

    lane = lax.broadcasted_iota(jnp.int32, (1, 128), 1)
    zero = jnp.bfloat16(0)
    qa[:, :128] = q_ref[...]
    qa[:, 128:] = l_ref[...]
    ga[:, :128] = g_ref[...]
    product = f32(g_ref[...]) * f32(o_ref[...])
    aug = 0.0
    for h in range(2):
        mine = head_lanes(h)
        inner = -jnp.sum(jnp.where(mine, product, 0.0), axis=1, keepdims=True)
        for i, part in enumerate(split3(inner)):
            aug = jnp.where(lane == 3 * h + i, part, aug)
        one = low(jnp.where((lane >= 3 * h) & (lane < 3 * h + 3), 1.0, 0.0))
        ka[h, :PADP, :128] = jnp.where(mine, pk_ref[...], zero)
        ka[h, PADP:, :128] = jnp.where(mine, k_ref[...], zero)
        va[h, :PADP, :128] = jnp.where(mine, pv_ref[...], zero)
        va[h, PADP:, :128] = jnp.where(mine, v_ref[...], zero)
        ka[h, :, 128:] = jnp.broadcast_to(one, (KY, 128))
        va[h, :, 128:] = jnp.broadcast_to(one, (KY, 128))
    ga[:, 128:] = low(aug)
    for i, (a, b, q0) in enumerate(KEY_BLOCKS):
        dk = dv = dqt = 0.0
        for h in range(2):
            mine = head_lanes(h)
            s = dg(ka[h, a:b, :], qa[q0:, :], NT)
            p = jnp.exp2(s * C2 + bias[a:b, q0:])
            dp = dg(va[h, a:b, :], ga[q0:, :], NT)
            ds = low(p * dp)
            dv += dg(low(p), jnp.where(mine, g_ref[q0:, :], zero), NN)
            dk += dg(ds, jnp.where(mine, q_ref[q0:, :], zero), NN)
            dqt += dg(ka[h, a:b, :128].T, ds, NN)
        if i == 0:
            dq[...] = dqt
            dk_ref[:256, :] = low(dk[PADP:] * SCALE)
            dv_ref[:256, :] = low(dv[PADP:])
        else:
            dq[:, q0:] += dqt
            dk_ref[q0 : q0 + 256, :] = low(dk * SCALE)
            dv_ref[q0 : q0 + 256, :] = low(dv)
    dq_ref[...] = low(dq[...].T * SCALE)


def attend_backward(qkv, prefix, edges, sums, hidden, ghid, first):
    pairs = qkv.shape[1] // 3 // 128
    width = pairs * 128
    blk = lambda off: pl.BlockSpec((LENGTH, 128), lambda h: (0, off + h))
    pblk = lambda off: pl.BlockSpec((PADP, 128), lambda h: (0, off + first + h))
    return pl.pallas_call(
        backward_kernel,
        grid=(pairs,),
        in_specs=[
            pl.BlockSpec((1, LENGTH), lambda h: (0, 0)),
            pl.BlockSpec((1, KX), lambda h: (0, 0)),
            blk(0), blk(pairs), blk(2 * pairs), pblk(0), pblk(ghid.shape[1] // 128), blk(0), blk(0),
            blk(first),
        ],
        out_specs=[blk(0)] * 3,
        out_shape=[jax.ShapeDtypeStruct((LENGTH, width), jnp.bfloat16)] * 3,
        scratch_shapes=[
            pltpu.VMEM((KY, LENGTH), jnp.float32),
            pltpu.VMEM((LENGTH, 256), jnp.bfloat16),
            pltpu.VMEM((LENGTH, 256), jnp.bfloat16),
            pltpu.VMEM((2, KY, 256), jnp.bfloat16),
            pltpu.VMEM((2, KY, 256), jnp.bfloat16),
            pltpu.VMEM((128, LENGTH), jnp.float32),
        ],
        compiler_params=params(),
    )(*edges, qkv, qkv, qkv, prefix, prefix, sums, hidden, ghid)


def prefix_kernel(
    qa_ref, qb_ref, sa_ref, sb_ref, oa_ref, ob_ref, g_ref, pk_ref, pv_ref,
    dk_ref, dv_ref, keys, values, ones, spots, dk_acc, dv_acc,
):
    i = pl.program_id(0)
    heads = keys.shape[0] // PADP
    depth = keys.shape[1]
    half = depth // 2
    col = lax.broadcasted_iota(jnp.int32, (1, depth), 1)

    @pl.when(i == 0)
    def _():
        zero = jnp.bfloat16(0)
        for h in range(heads):
            r = slice(PADP * h, PADP * h + PADP)
            mine = (col >= HEAD * h) & (col < HEAD * h + HEAD)
            keys[r, :] = jnp.where(mine, pk_ref[...], zero)
            values[r, :] = jnp.where(mine, pv_ref[...], zero)
            ones[r, :] = jnp.broadcast_to(low(jnp.where(mine, 1.0, 0.0)), (PADP, depth))
            start = 128 * (h // 2) + 3 * (h % 2)
            spot = (col >= start) & (col < start + 3)
            spots[r, :] = jnp.broadcast_to(low(jnp.where(spot, 1.0, 0.0)), (PADP, depth))
        dk_acc[...] = jnp.zeros_like(dk_acc)
        dv_acc[...] = jnp.zeros_like(dv_acc)

    lane = lax.broadcasted_iota(jnp.int32, (1, PADP * heads), 1)
    g = g_ref[...]
    s = dg(qa_ref[...], keys[:, :half], NT) + dg(qb_ref[...], keys[:, half:], NT)
    s += dg(sa_ref[...], spots[:, :half], NT) + dg(sb_ref[...], spots[:, half:], NT)
    p = jnp.where(lane % PADP < PREFIX, jnp.exp2(s * C2), 0.0)
    dp = dg(g, values[...], NT)
    for c, o_ref in ((0, oa_ref), (half, ob_ref)):
        product = f32(g[:, c : c + half]) * f32(o_ref[...])
        high = low(product)
        dp -= dg(high, ones[:, c : c + half], NT)
        dp -= dg(low(product - f32(high)), ones[:, c : c + half], NT)
    ds = low(p * dp)
    dk_acc[:, :half] += dg(ds, qa_ref[...], TN)
    dk_acc[:, half:] += dg(ds, qb_ref[...], TN)
    dv_acc[...] += dg(low(p), g, TN)

    @pl.when(i == pl.num_programs(0) - 1)
    def _():
        dk = dv = 0.0
        for h in range(heads):
            r = slice(PADP * h, PADP * h + PADP)
            mine = (col >= HEAD * h) & (col < HEAD * h + HEAD)
            dk += jnp.where(mine, dk_acc[r, :], 0.0)
            dv += jnp.where(mine, dv_acc[r, :], 0.0)
        dk_ref[...] = dk * SCALE
        dv_ref[...] = dv


def prefix_call(qkv, sums, hidden, ghid, prefix, block=256):
    rows, depth = ghid.shape
    half = depth // 2
    heads = depth // HEAD
    row = lambda w: pl.BlockSpec((block, w), lambda i: (i, 0))
    whole = lambda c: pl.BlockSpec((PADP, depth), lambda i: (0, c))
    return pl.pallas_call(
        prefix_kernel,
        grid=(rows // block,),
        in_specs=[row(half)] * 6 + [row(depth), whole(0), whole(1)],
        out_specs=[whole(0)] * 2,
        out_shape=[jax.ShapeDtypeStruct((PADP, depth), jnp.float32)] * 2,
        scratch_shapes=[pltpu.VMEM((PADP * heads, depth), jnp.bfloat16)] * 4
        + [pltpu.VMEM((PADP * heads, depth), jnp.float32)] * 2,
        compiler_params=params(),
    )(*qkv, *sums, *hidden, ghid, prefix, prefix)


def tree_sum(values):
    while len(values) > 1:
        values = [values[i] + values[i + 1] for i in range(0, len(values), 2)]
    return values[0]


def make_body(dp, fsdp):
    staged = dp == 8 and fsdp == 4

    def body(
        tokens, segments, cotangent, ln1_gain, ln1_bias, w_qkv, b_qkv, w_out, b_out,
        ln2_gain, ln2_bias, w_fc, b_fc, w_proj, b_proj, prefix_embed, w_mid, b_mid, w_kv, b_kv,
    ):
        depth = tokens.shape[1]
        half = depth // 2
        pairs = half // 128
        small = [ln1_gain, ln1_bias, b_out, ln2_gain, ln2_bias, b_proj, b_qkv, b_fc]
        widths = [one.shape[0] for one in small]
        shard_a = jnp.concatenate([w_qkv[:, i * depth : i * depth + half] for i in range(3)], 1)
        shard_b = jnp.concatenate(
            [w_qkv[:, i * depth + half : (i + 1) * depth] for i in range(3)] + [w_out], 1
        )
        if staged:
            order = place_order(dp, fsdp)
            za, shard_b, small = fence(z_stage(shard_a, fsdp), shard_b, small)
            smalls = gather_small(small, dp * fsdp)
            near, far = glue(*za)
            xa, zb, w_fc, smalls, segments, prefix_embed, w_proj = fence(
                first_stage(near, far, dp), z_stage(shard_b, fsdp), w_fc, smalls, segments,
                prefix_embed, w_proj,
            )
            ya = second_stage(*join_stage(xa), dp)
            xb = first_stage(*glue(*zb), dp)
            zf = jnp.concatenate([w_fc[None], flip_z(w_fc[None], 2, fsdp)], 0)
            proj = lax.all_gather(w_proj, AXES, axis=0, tiled=True)
        else:
            order = jnp.arange(PIECES, dtype=jnp.int32)
            smalls = gather_small(small, dp * fsdp)
            pieces_a, pieces_b, pieces_f = (natural_pieces(a) for a in (shard_a, shard_b, w_fc))
            proj = lax.all_gather(w_proj, AXES, axis=0, tiled=True)
        embed_pad = jnp.pad(prefix_embed, ((0, PADP - PREFIX), (0, 0)))
        vectors, bias_a, bias_b, fc_bias = unpack_call(smalls, widths, depth, w_fc.shape[1])
        mid_act, prefix_kv = adapter_call(embed_pad, w_mid, b_mid, w_kv, b_kv)
        edges = segment_edges(segments)
        if staged:
            ready = (order, edges, vectors, bias_a, bias_b, fc_bias, prefix_kv, mid_act)
            ya, xb, zf, ready = fence(ya, xb, zf, ready)
            order, edges, vectors, bias_a, bias_b, fc_bias, prefix_kv, mid_act = ready
            pieces_a = core_stage(ya, dp)
            yb = second_stage(*join_stage(xb), dp)
            far = flip_z(zf, 1, fsdp)
        hidden_a, sums_a, qkv_a, weight_a = front_call(
            order, edges, tokens, vectors, bias_a, prefix_kv, 0, pieces_a
        )
        if staged:
            hidden_a, yb, far = fence(hidden_a, yb, far)
            pieces_b = core_stage(yb, dp)
            xf = first_stage(zf, far, dp)
        hidden_b, sums_b, qkv_b, weight_b = front_call(
            order, edges, tokens, vectors, bias_b, prefix_kv, pairs, pieces_b
        )
        if staged:
            hidden_b, xf = fence(hidden_b, xf)
            hidden_b, nearfar = fence(hidden_b, join_stage(xf))
            yf = second_stage(*nearfar, dp)
        mixed, normed_two, wout = out_call(
            order, tokens, hidden_a, hidden_b, vectors, pieces_b, 3 * half
        )
        gact = gact_call(cotangent, proj)
        if staged:
            gact, yf = fence(gact, yf)
            pieces_f = core_stage(yf, dp)
        block_out, gmix, ghid = ffn_call(
            order, normed_two, cotangent, gact, fc_bias, mixed, vectors, wout, proj, pieces_f
        )
        dpk, dpv = prefix_call((qkv_a, qkv_b), (sums_a, sums_b), (hidden_a, hidden_b), ghid, prefix_kv)
        total = jnp.concatenate([dpk, dpv], 1)
        if staged:
            total, ghid = fence(total, ghid)
            spread = [total] + [
                lax.ppermute(total, "fsdp", [(i, i ^ m) for i in range(fsdp)]) for m in (1, 2, 3)
            ]
        gqa, gka, gva = attend_backward(qkv_a, prefix_kv, edges, sums_a, hidden_a, ghid, 0)
        if staged:
            gqa, spread, ghid = fence(gqa, spread, ghid)
            total = tree_sum(spread)
            total, ghid = fence(total, ghid)
            spread = [total] + [flip_dp(total, m, dp) for m in (1, 2, 3)]
        gqb, gkb, gvb = attend_backward(qkv_b, prefix_kv, edges, sums_b, hidden_b, ghid, pairs)
        if staged:
            gqb, spread = fence(gqb, spread)
            total = tree_sum(spread)
            gqb, total = fence(gqb, total)
            other = flip_dp(total, 4, dp)
        else:
            total = lax.psum(total, AXES)
            other = jnp.zeros_like(total)
        grad_tokens = final_call(
            tokens, gmix, vectors, weight_a, weight_b, (gqa, gka, gva, gqb, gkb, gvb)
        )
        adapter = adapter_back_call(total, other, embed_pad, w_mid, w_kv, mid_act)
        return (block_out, grad_tokens) + adapter

    return body


def solution(mesh):
    dp, fsdp = mesh.shape["dp"], mesh.shape["fsdp"]
    rows, flat = P(AXES, None), P(AXES)
    return jax.shard_map(
        make_body(dp, fsdp),
        mesh=mesh,
        in_specs=(
            rows, flat, rows, flat, flat, rows, flat, rows, flat, flat, flat, rows, flat, rows,
            flat, P(), P(), P(), P(), P(),
        ),
        out_specs=(rows, rows, P(), P(), P(), P(), P()),
        check_vma=False,
    )
```

```python
import jax
import jax.numpy as jnp
from jax import lax
from jax.experimental import pallas as pl
from jax.experimental.pallas import tpu as pltpu
from jax.sharding import PartitionSpec as P

HEAD = 64
PREFIX = 10
PADP = 16
LENGTH = 1024
AXES = ("dp", "fsdp")
LOG2E = 1.4426950408889634
SCALE = HEAD**-0.5
C2 = SCALE * LOG2E
NEG = -1e30
KX = 1152
KY = PADP + LENGTH
NT = (((1,), (1,)), ((), ()))
NN = (((1,), (0,)), ((), ()))
TN = (((0,), (0,)), ((), ()))
PIECES = 32
MB = 1024 * 1024


def dg(left, right, dims):
    return lax.dot_general(left, right, dims, preferred_element_type=jnp.float32)


def f32(value):
    return value.astype(jnp.float32)


def low(value):
    return value.astype(jnp.bfloat16)


def params():
    return pltpu.CompilerParams(vmem_limit_bytes=60 * MB)


def flip_dp(value, mask, size):
    return lax.ppermute(value, "dp", [(i, i ^ mask) for i in range(size)])


def flip_z(value, mask, size):
    return lax.ppermute(value, "fsdp", [(i, i ^ mask) for i in range(size)])


def fence(*values):
    return lax.optimization_barrier(values)


def z_stage(shard, fsdp):
    own = shard[None]
    return [own] + [flip_z(own, m, fsdp) for m in (2, 1, 3)]


def first_stage(near, far, dp):
    return near, far, flip_dp(near, 2, dp), flip_dp(far, 4, dp)


def direct_order(dp, fsdp):
    d = lax.axis_index("dp")
    z = lax.axis_index("fsdp")
    places = []
    for core in (0, 1):
        for mask in (0, 2, 4, 6):
            places += [(d ^ (core ^ mask)) * fsdp + (z ^ turn) for turn in (0, 2, 1, 3)]
    return jnp.stack(places).astype(jnp.int32)


def glue_kernel(a_ref, b_ref, c_ref, d_ref, near_ref, far_ref):
    size = a_ref.shape[0]
    near_ref[:size] = a_ref[...]
    near_ref[size:] = b_ref[...]
    far_ref[:size] = c_ref[...]
    far_ref[size:] = d_ref[...]


def glue(a, b, c, d):
    vmem = pl.BlockSpec(memory_space=pltpu.VMEM)
    shape = (2 * a.shape[0],) + a.shape[1:]
    return pl.pallas_call(
        glue_kernel,
        in_specs=[vmem] * 4,
        out_specs=[vmem] * 2,
        out_shape=[jax.ShapeDtypeStruct(shape, a.dtype)] * 2,
    )(a, b, c, d)


def join_stage(state):
    return glue(state[0], state[2], state[1], state[3])


def second_stage(near, far, dp):
    return [near, flip_dp(near, 4, dp), far, flip_dp(far, 2, dp)]


def core_stage(plane, dp):
    return plane + [flip_dp(one, 1, dp) for one in plane]


def place_order(dp, fsdp):
    d = lax.axis_index("dp")
    z = lax.axis_index("fsdp")
    places = []
    for core in (0, 1):
        for first, second, base in ((2, 4, 0), (4, 2, 1)):
            for outer in (0, second):
                for inner in (0, first):
                    for turn in (base, base ^ 2):
                        places.append((d ^ (core ^ outer ^ inner)) * fsdp + (z ^ turn))
    return jnp.stack(places).astype(jnp.int32)


SMALL = 8


def pack_kernel(*refs):
    ins, out_ref = refs[:SMALL], refs[SMALL]
    row = jnp.zeros((SMALL, 128), jnp.float32)
    spot = lax.broadcasted_iota(jnp.int32, (SMALL, 128), 0)
    for i, one in enumerate(ins):
        wide = one.shape[1]
        value = f32(one[...])
        if wide < 128:
            value = jnp.concatenate([value, jnp.zeros((1, 128 - wide), jnp.float32)], 1)
        row = jnp.where(spot == i, value, row)
    out_ref[...] = jnp.broadcast_to(low(row)[None], out_ref.shape)


def pack_call(small, devices):
    vmem = pl.BlockSpec(memory_space=pltpu.VMEM)
    return pl.pallas_call(
        pack_kernel,
        in_specs=[vmem] * SMALL,
        out_specs=vmem,
        out_shape=jax.ShapeDtypeStruct((devices, SMALL, 128), jnp.bfloat16),
    )(*[one[None] for one in small])


def unpack_kernel(widths, all_ref, rows_ref, qa_ref, qb_ref, fc_ref):
    devices = all_ref.shape[0]
    depth = rows_ref.shape[1]
    half = depth // 2

    def spread(i, place):
        share = all_ref[:, i, :]
        lane = lax.broadcasted_iota(jnp.int32, (128, place.shape[1]), 0)
        pick = low(jnp.where(lane == place % widths[i], 1.0, 0.0))
        owner = lax.broadcasted_iota(jnp.int32, (devices, place.shape[1]), 0)
        found = jnp.where(owner == place // widths[i], dg(share, pick, NN), 0.0)
        return jnp.sum(found, axis=0, keepdims=True)

    natural = lax.broadcasted_iota(jnp.int32, (1, depth), 1)
    for i in range(SMALL - 2):
        rows_ref[i : i + 1, :] = spread(i, natural)
    rows_ref[SMALL - 2 :, :] = jnp.zeros((2, depth), jnp.float32)
    short = lax.broadcasted_iota(jnp.int32, (1, half), 1)
    for k in range(3):
        qa_ref[:, k * half : (k + 1) * half] = spread(SMALL - 2, short + k * depth)
        qb_ref[:, k * half : (k + 1) * half] = spread(SMALL - 2, short + k * depth + half)
    for k in range(fc_ref.shape[1] // depth):
        fc_ref[:, k * depth : (k + 1) * depth] = spread(SMALL - 1, natural + k * depth)


def unpack_call(gathered, widths, depth, wide):
    vmem = pl.BlockSpec(memory_space=pltpu.VMEM)
    shapes = ((SMALL, depth), (1, 3 * depth // 2), (1, 3 * depth // 2), (1, wide))
    return pl.pallas_call(
        lambda *refs: unpack_kernel(widths, *refs),
        in_specs=[vmem],
        out_specs=[vmem] * 4,
        out_shape=[jax.ShapeDtypeStruct(shape, jnp.float32) for shape in shapes],
    )(gathered)


def adapter_kernel(embed_ref, wm_ref, bm_ref, wkv_ref, bkv_ref, mid_ref, kv_ref):
    mid = jnp.tanh(dg(embed_ref[...], wm_ref[...], NN) + f32(bm_ref[...]))
    mid_ref[...] = mid
    kv = low(dg(low(mid), wkv_ref[...], NN) + f32(bkv_ref[...]))
    row = lax.broadcasted_iota(jnp.int32, kv.shape, 0)
    kv_ref[...] = jnp.where(row < PREFIX, kv, jnp.bfloat16(0))


def adapter_call(embed, w_mid, b_mid, w_kv, b_kv):
    vmem = pl.BlockSpec(memory_space=pltpu.VMEM)
    return pl.pallas_call(
        adapter_kernel,
        in_specs=[vmem] * 5,
        out_specs=[vmem] * 2,
        out_shape=[
            jax.ShapeDtypeStruct((PADP, w_mid.shape[1]), jnp.float32),
            jax.ShapeDtypeStruct((PADP, w_kv.shape[1]), jnp.bfloat16),
        ],
    )(embed, w_mid, b_mid[None], w_kv, b_kv[None])


def adapter_back_kernel(
    own_ref, other_ref, embed_ref, wm_ref, wkv_ref, mid_ref, ge_ref, gmw_ref, gmb_ref, gkw_ref, gkb_ref
):
    low_sum = low(own_ref[...] + other_ref[...])
    mid = mid_ref[...]
    gkw_ref[...] = dg(low(mid), low_sum, TN)
    gkb_ref[...] = jnp.sum(f32(low_sum), axis=0, keepdims=True)
    grad = low(dg(low_sum, wkv_ref[...], NT) * (1.0 - mid * mid))
    gmw_ref[...] = dg(embed_ref[...], grad, TN)
    gmb_ref[...] = jnp.sum(f32(grad), axis=0, keepdims=True)
    ge_ref[...] = dg(grad, wm_ref[...], NT)[:PREFIX]


def adapter_back_call(own, other, embed, w_mid, w_kv, mid):
    vmem = pl.BlockSpec(memory_space=pltpu.VMEM)
    depth, middle = w_mid.shape
    shapes = ((PREFIX, depth), (depth, middle), (1, middle), w_kv.shape, (1, w_kv.shape[1]))
    found = pl.pallas_call(
        adapter_back_kernel,
        in_specs=[vmem] * 6,
        out_specs=[vmem] * 5,
        out_shape=[jax.ShapeDtypeStruct(shape, jnp.float32) for shape in shapes],
    )(own, other, embed, w_mid, w_kv, mid)
    return found[0], found[1], found[2][0], found[3], found[4][0]


def gather_small(small, devices):
    return lax.all_to_all(pack_call(small, devices), AXES, 0, 0, tiled=True)


def natural_pieces(shard):
    whole = lax.all_gather(shard, AXES, axis=0, tiled=True)
    whole = whole.reshape(8, 4, whole.shape[0] // PIECES, *whole.shape[1:])
    return [whole[i] for i in range(8)]


def place_pieces(order_ref, piece_refs, target_ref, columns, sems):
    copies = []
    for b in range(8):
        for k in range(4):
            i = b * 4 + k
            row = pl.multiple_of(order_ref[i] * PIECES, PIECES)
            copies.append(
                pltpu.make_async_copy(
                    piece_refs[b].at[k, :, columns],
                    target_ref.at[pl.ds(row, PIECES), :],
                    sems.at[i],
                )
            )
    return copies


def anyspec():
    return pl.BlockSpec(memory_space=pl.ANY)


def smem():
    return pl.BlockSpec(memory_space=pltpu.SMEM)


def norm_rows(values):
    mean = jnp.mean(values, axis=-1, keepdims=True)
    centred = values - mean
    spread = jnp.mean(centred * centred, axis=-1, keepdims=True)
    return centred * lax.rsqrt(spread + 1e-05), spread


def norm_pull(values, gain_row, grad):
    unit, spread = norm_rows(values)
    weighted = grad * gain_row
    first = jnp.mean(weighted, axis=-1, keepdims=True)
    second = jnp.mean(weighted * unit, axis=-1, keepdims=True)
    return (weighted - first - unit * second) * lax.rsqrt(spread + 1e-05)


HIDDEN = 512


def out_kernel(
    column, order_ref, tokens_ref, ha_ref, hb_ref, vec_ref, cot_ref, proj_ref, *rest
):
    pieces, (mixed_ref, normed_ref, gact_ref, weight_ref, sems) = rest[:8], rest[8:]

    def copies():
        width = weight_ref.shape[1]
        return place_pieces(order_ref, pieces, weight_ref, pl.ds(column, width), sems)

    @pl.when(pl.program_id(0) == 0)
    def _():
        for one in copies():
            one.start()
        for one in copies():
            one.wait()

    gact_ref[0] = low(dg(cot_ref[...], proj_ref[...], NT))
    half = ha_ref.shape[1]
    mixed = f32(tokens_ref[...]) + vec_ref[2:3, :]
    mixed += dg(ha_ref[...], weight_ref[:half, :], NN)
    mixed += dg(hb_ref[...], weight_ref[half:, :], NN)
    mixed_ref[...] = mixed
    unit, _ = norm_rows(mixed)
    normed_ref[...] = low(unit * vec_ref[3:4, :] + vec_ref[4:5, :])


def out_call(order, tokens, hidden_a, hidden_b, vectors, cot, proj, pieces, column):
    rows, depth = tokens.shape
    blocks = proj.shape[0] // HIDDEN
    row = lambda w: pl.BlockSpec((rows // blocks, w), lambda j: (j, 0))
    whole = lambda s: pl.BlockSpec(s, lambda j: (0, 0))
    return pl.pallas_call(
        lambda *refs: out_kernel(column, *refs),
        grid=(blocks,),
        in_specs=[smem(), row(depth), row(depth // 2), row(depth // 2), whole(vectors.shape)]
        + [whole(cot.shape), pl.BlockSpec((HIDDEN, depth), lambda j: (j, 0))]
        + [anyspec()] * 8,
        out_specs=[
            row(depth),
            row(depth),
            pl.BlockSpec((1, rows, HIDDEN), lambda j: (j, 0, 0)),
            whole((depth, depth)),
        ],
        out_shape=[
            jax.ShapeDtypeStruct((rows, depth), jnp.float32),
            jax.ShapeDtypeStruct((rows, depth), jnp.bfloat16),
            jax.ShapeDtypeStruct((blocks, rows, HIDDEN), jnp.bfloat16),
            jax.ShapeDtypeStruct((depth, depth), jnp.bfloat16),
        ],
        scratch_shapes=[pltpu.SemaphoreType.DMA((PIECES,))],
        compiler_params=params(),
    )(order, tokens, hidden_a, hidden_b, vectors, cot, proj, *pieces)


GELU_A = 0.7978845608028654
GELU_B = 0.044715


def gelu_pair(value):
    square = value * value
    half = 0.5 + 0.5 * jnp.tanh(value * (GELU_A + GELU_A * GELU_B * square))
    act = value * half
    slope = half + 2.0 * act * (1.0 - half) * (GELU_A + 3.0 * GELU_A * GELU_B * square)
    return act, slope


def ffn_kernel(
    order_ref, bias_ref, vec_ref, normed_hbm, gact_hbm, proj_hbm, mixed_hbm, cot_hbm, wout_hbm, *rest
):
    pieces, (block_hbm, gmix_hbm, ghid_hbm) = rest[:8], rest[8:11]
    normed, gact, fc, proj, pre, act, gpre, acc_ref, gacc_ref = rest[11:20]
    nsem, gsem, psem, fsem, tsem, osem = rest[20:]
    blocks = gact.shape[0]
    wide = blocks * HIDDEN // 2

    def columns(half):
        found = []
        for p in range(PIECES):
            row = pl.multiple_of(order_ref[p] * PIECES, PIECES)
            source = pieces[p // 4].at[p % 4, :, pl.ds(half * wide, wide)]
            target = fc.at[pl.ds(row, PIECES), pl.ds(half * wide, wide)]
            found.append(pltpu.make_async_copy(source, target, fsem.at[half, p]))
        return found

    def gact_copy(j):
        return pltpu.make_async_copy(gact_hbm.at[j], gact.at[j], gsem.at[j])

    def proj_copy(j):
        rows = pl.ds(pl.multiple_of(j * HIDDEN, HIDDEN), HIDDEN)
        return pltpu.make_async_copy(proj_hbm.at[rows, :], proj.at[rows, :], psem.at[j])

    def step(j, slot, first, second, third):
        if first:
            c = pl.ds(pl.multiple_of(j * HIDDEN, HIDDEN), HIDDEN)
            pre[slot] = dg(normed[...], fc[:, c], NN) + bias_ref[:, c]
        if second:
            value, slope = gelu_pair(pre[1 - slot])
            act[1 - slot] = low(value)
            gpre[1 - slot] = low(f32(gact[j - 1]) * slope)
        if third:
            c = pl.ds(pl.multiple_of((j - 2) * HIDDEN, HIDDEN), HIDDEN)
            acc_ref[...] += dg(act[slot], proj[c, :], NN)
            gacc_ref[...] += dg(gpre[slot], fc[:, c], NT)

    start = pltpu.make_async_copy(normed_hbm, normed, nsem)
    start.start()
    for one in columns(0):
        one.start()
    gact_copy(0).start()
    for one in columns(1):
        one.start()
    for j in range(blocks):
        if j > 0:
            gact_copy(j).start()
        proj_copy(j).start()
    acc_ref[...] = jnp.zeros_like(acc_ref)
    gacc_ref[...] = jnp.zeros_like(gacc_ref)
    start.wait()
    for one in columns(0):
        one.wait()
    step(0, 0, True, False, False)
    gact_copy(0).wait()
    step(1, 1, True, True, False)
    for one in columns(1):
        one.wait()
    for j in range(blocks):
        if j > 0:
            gact_copy(j).wait()
        proj_copy(j).wait()

    def pair(k, carry):
        for i in (0, 1):
            step(2 * k + 2 + i, i, True, True, True)
        return carry

    lax.fori_loop(0, blocks // 2 - 1, pair, 0)
    sides = [pl.ds(k * HIDDEN, HIDDEN) for k in (0, 1)]
    late = [pltpu.make_async_copy(cot_hbm, normed, tsem.at[0])]
    for k, c in enumerate(sides):
        late.append(pltpu.make_async_copy(wout_hbm.at[:, c], gact.at[k], tsem.at[1 + k]))
    for one in late:
        one.start()
    step(blocks, 0, False, True, True)
    for k, c in enumerate(sides):
        late.append(pltpu.make_async_copy(mixed_hbm.at[:, c], pre.at[k], tsem.at[3 + k]))
        late[-1].start()
    step(blocks + 1, 1, False, False, True)
    for one in late:
        one.wait()
    outs = []
    size = normed.shape[0] // 4
    for i in range(4):
        r = slice(i * size, (i + 1) * size)
        value = jnp.concatenate([pre[0, r, :], pre[1, r, :]], 1)
        block = low(value + acc_ref[r, :] + vec_ref[5:6, :])
        gmix = f32(normed[r, :]) + norm_pull(value, vec_ref[3:4, :], gacc_ref[r, :])
        gmix_low = low(gmix)
        ghid = dg(gmix_low[:, :HIDDEN], gact[0], NT) + dg(gmix_low[:, HIDDEN:], gact[1], NT)
        for k, c in enumerate((slice(0, HIDDEN), slice(HIDDEN, 2 * HIDDEN))):
            act[k, r, :] = block[:, c]
            pre[k, r, :] = gmix[:, c]
            gpre[k, r, :] = low(ghid[:, c])
            for m, (source, target) in enumerate(
                ((act, block_hbm), (pre, gmix_hbm), (gpre, ghid_hbm))
            ):
                spot = target.at[r, sides[k]]
                copy = pltpu.make_async_copy(source.at[k, r, :], spot, osem.at[i, k, m])
                copy.start()
                outs.append(copy)
    for one in outs:
        one.wait()


def ffn_call(order, normed, gact, bias, proj, mixed, cot, vectors, wout, pieces):
    rows, depth = normed.shape
    blocks = gact.shape[0]
    wide = blocks * HIDDEN
    vmem = pl.BlockSpec(memory_space=pltpu.VMEM)
    return pl.pallas_call(
        ffn_kernel,
        in_specs=[smem(), vmem, vmem] + [anyspec()] * 14,
        out_specs=[anyspec()] * 3,
        out_shape=[
            jax.ShapeDtypeStruct((rows, depth), jnp.bfloat16),
            jax.ShapeDtypeStruct((rows, depth), jnp.float32),
            jax.ShapeDtypeStruct((rows, depth), jnp.bfloat16),
        ],
        scratch_shapes=[
            pltpu.VMEM((rows, depth), jnp.bfloat16),
            pltpu.VMEM(gact.shape, jnp.bfloat16),
            pltpu.VMEM((depth, wide), jnp.bfloat16),
            pltpu.VMEM((wide, depth), jnp.bfloat16),
            pltpu.VMEM((2, rows, HIDDEN), jnp.float32),
            pltpu.VMEM((2, rows, HIDDEN), jnp.bfloat16),
            pltpu.VMEM((2, rows, HIDDEN), jnp.bfloat16),
            pltpu.VMEM((rows, depth), jnp.float32),
            pltpu.VMEM((rows, depth), jnp.float32),
            pltpu.SemaphoreType.DMA,
            pltpu.SemaphoreType.DMA((blocks,)),
            pltpu.SemaphoreType.DMA((blocks,)),
            pltpu.SemaphoreType.DMA((2, PIECES)),
            pltpu.SemaphoreType.DMA((5,)),
            pltpu.SemaphoreType.DMA((4, 2, 3)),
        ],
        compiler_params=params(),
    )(order, bias, vectors, normed, gact, proj, mixed, cot, wout, *pieces)


def final_kernel(tokens_ref, gmix_ref, vec_ref, wa_ref, wb_ref, *rest):
    grads, out_ref = rest[:6], rest[6]
    total = None
    for i in range(6):
        half = grads[i].shape[1]
        c = (i % 3) * half
        weight = (wa_ref if i < 3 else wb_ref)[:, c : c + half]
        part = dg(grads[i][...], weight, NT)
        total = part if total is None else total + part
    pulled = norm_pull(f32(tokens_ref[...]), vec_ref[0:1, :], total)
    out_ref[...] = low(gmix_ref[...] + pulled)


def final_call(tokens, gmix, vectors, wa, wb, grads, block=256):
    rows, depth = tokens.shape
    row = lambda w: pl.BlockSpec((block, w), lambda i: (i, 0))
    whole = lambda s: pl.BlockSpec(s, lambda i: (0, 0))
    return pl.pallas_call(
        final_kernel,
        grid=(rows // block,),
        in_specs=[row(depth), row(depth), whole(vectors.shape), whole(wa.shape), whole(wb.shape)]
        + [row(grads[0].shape[1])] * 6,
        out_specs=row(depth),
        out_shape=jax.ShapeDtypeStruct((rows, depth), jnp.bfloat16),
        compiler_params=params(),
    )(tokens, gmix, vectors, wa, wb, *grads)


def split3(value):
    high = f32(low(value))
    rest = value - high
    middle = f32(low(rest))
    return high, middle, rest - middle


QUERY_BLOCKS = ((0, 240, 256), (240, 496, 512), (496, 752, 768), (752, 1024, 1152))
KEY_BLOCKS = ((0, 272, 0), (272, 528, 256), (528, 784, 512), (784, 1040, 768))


def lane_pieces(value):
    lane = lax.broadcasted_iota(jnp.int32, (1, 128), 1)
    high, middle, rest = split3(value)
    picked = jnp.where(lane % 3 == 0, high, jnp.where(lane % 3 == 1, middle, rest))
    return low(jnp.where(lane < 6, picked, 0.0))


def head_spots():
    row = lax.broadcasted_iota(jnp.int32, (128, 128), 0)
    col = lax.broadcasted_iota(jnp.int32, (128, 128), 1)
    return low(jnp.where((row // HEAD == col // 3) & (col < 6), 1.0, 0.0))


def as_column(row):
    return jnp.broadcast_to(f32(row), (8, row.shape[1])).T[:, 0:1].astype(jnp.int32)


def head_lanes(h):
    lane = lax.broadcasted_iota(jnp.int32, (1, 128), 1)
    return (lane >= HEAD * h) & (lane < HEAD * h + HEAD)


def front_kernel(
    order_ref, seg_ref, keys_ref, tokens_ref, vec_ref, qb_ref, pk_ref, pv_ref, *rest
):
    pieces, (o_ref, l_ref, qkv_ref, weight_ref, bias, kx, vx, normed, sems) = rest[:8], rest[8:]
    step = pl.program_id(0)
    width = weight_ref.shape[1]

    @pl.when(step == 0)
    def _():
        copies = place_pieces(order_ref, pieces, weight_ref, pl.ds(0, width), sems)
        for one in copies:
            one.start()
        row = lax.broadcasted_iota(jnp.int32, (LENGTH, KX), 0) + PADP
        col = lax.broadcasted_iota(jnp.int32, (LENGTH, KX), 1)
        seen = ((as_column(seg_ref[...]) == keys_ref[...]) & (col <= row)) | (col < PREFIX)
        bias[...] = jnp.where(seen, 0.0, NEG)
        unit, _ = norm_rows(f32(tokens_ref[...]))
        normed[...] = low(unit * vec_ref[0:1, :] + vec_ref[1:2, :])
        kx[...] = jnp.zeros_like(kx)
        vx[...] = jnp.zeros_like(vx)
        for h in range(2):
            vx[h, :, 128:] = jnp.ones((KX, 128), jnp.bfloat16)
        for one in copies:
            one.wait()
        for c in range(0, width, 512):
            part = dg(normed[...], weight_ref[:, c : c + 512], NN) + qb_ref[:, c : c + 512]
            qkv_ref[:, c : c + 512] = low(part)

    lane = lax.broadcasted_iota(jnp.int32, (1, 128), 1)
    zero = jnp.bfloat16(0)
    at = [pl.ds(pl.multiple_of(i * (width // 3) + step * 128, 128), 128) for i in range(3)]
    for h in range(2):
        mine = head_lanes(h)
        kx[h, :PADP, :] = jnp.where(mine, pk_ref[...], zero)
        kx[h, PADP:KY, :] = jnp.where(mine, qkv_ref[:, at[1]], zero)
        vx[h, :PADP, :128] = jnp.where(mine, pv_ref[...], zero)
        vx[h, PADP:KY, :128] = jnp.where(mine, qkv_ref[:, at[2]], zero)
    for a, b, nk in QUERY_BLOCKS:
        outs, sums = [], []
        for h in range(2):
            s = dg(qkv_ref[a:b, at[0]], kx[h, :nk, :], NT) * C2 + bias[a:b, :nk]
            top = jnp.max(s, axis=1, keepdims=True)
            o = dg(low(jnp.exp2(s - top)), vx[h, :nk, :], NN)
            mass = o[:, 128:]
            outs.append(o[:, :128] / mass)
            sums.append((top + jnp.log2(mass)) * (-1.0 / C2))
        o_ref[a:b, :] = low(outs[0] + outs[1])
        aug = 0.0
        for i, part in enumerate(split3(sums[0]) + split3(sums[1])):
            aug = jnp.where(lane == i, part, aug)
        l_ref[a:b, :] = low(aug)


def segment_edges(segments):
    keys = jnp.pad(segments, (PADP, KX - KY), constant_values=-1)
    return segments[None, :], keys[None, :]


def front_call(order, edges, tokens, vectors, qkv_bias, prefix, first, pieces):
    depth = tokens.shape[1]
    width = qkv_bias.shape[1]
    pairs = width // 3 // 128
    whole = lambda s: pl.BlockSpec(s, lambda h: (0, 0), pipeline_mode=pl.Buffered(1))
    blk = pl.BlockSpec((LENGTH, 128), lambda h: (0, h))
    pblk = lambda off: pl.BlockSpec((PADP, 128), lambda h: (0, off + first + h))
    return pl.pallas_call(
        front_kernel,
        grid=(pairs,),
        in_specs=[smem(), whole((1, LENGTH)), whole((1, KX)), whole(tokens.shape)]
        + [whole(vectors.shape), whole(qkv_bias.shape), pblk(0), pblk(depth // 128)]
        + [anyspec()] * 8,
        out_specs=[blk, blk, whole((LENGTH, width)), whole((depth, width))],
        out_shape=[jax.ShapeDtypeStruct((LENGTH, width // 3), jnp.bfloat16)] * 2
        + [
            jax.ShapeDtypeStruct((LENGTH, width), jnp.bfloat16),
            jax.ShapeDtypeStruct((depth, width), jnp.bfloat16),
        ],
        scratch_shapes=[
            pltpu.VMEM((LENGTH, KX), jnp.float32),
            pltpu.VMEM((2, KX, 128), jnp.bfloat16),
            pltpu.VMEM((2, KX, 256), jnp.bfloat16),
            pltpu.VMEM(tokens.shape, jnp.bfloat16),
            pltpu.SemaphoreType.DMA((PIECES,)),
        ],
        compiler_params=params(),
    )(order, *edges, tokens, vectors, qkv_bias, prefix, prefix, *pieces)


def backward_kernel(
    seg_ref, keys_ref, q_ref, k_ref, v_ref, pk_ref, pv_ref, l_ref, o_ref, g_ref,
    dq_ref, dk_ref, dv_ref, bias, qa, ga, ka, va, dq,
):
    @pl.when(pl.program_id(0) == 0)
    def _():
        row = lax.broadcasted_iota(jnp.int32, (KY, LENGTH), 0)
        col = lax.broadcasted_iota(jnp.int32, (KY, LENGTH), 1) + PADP
        keys = as_column(keys_ref[...])[:KY]
        seen = ((keys == seg_ref[...]) & (row <= col)) | (row < PREFIX)
        bias[...] = jnp.where(seen, 0.0, NEG)

    lane = lax.broadcasted_iota(jnp.int32, (1, 128), 1)
    zero = jnp.bfloat16(0)
    qa[:, :128] = q_ref[...]
    qa[:, 128:] = l_ref[...]
    ga[:, :128] = g_ref[...]
    product = f32(g_ref[...]) * f32(o_ref[...])
    high = low(product)
    spots = head_spots()
    inner = dg(high, spots, NN) + dg(low(product - f32(high)), spots, NN)
    ga[:, 128:] = lane_pieces(-inner)
    for h in range(2):
        mine = head_lanes(h)
        one = low(jnp.where((lane >= 3 * h) & (lane < 3 * h + 3), 1.0, 0.0))
        ka[h, :PADP, :128] = jnp.where(mine, pk_ref[...], zero)
        ka[h, PADP:, :128] = jnp.where(mine, k_ref[...], zero)
        va[h, :PADP, :128] = jnp.where(mine, pv_ref[...], zero)
        va[h, PADP:, :128] = jnp.where(mine, v_ref[...], zero)
        ka[h, :, 128:] = jnp.broadcast_to(one, (KY, 128))
        va[h, :, 128:] = jnp.broadcast_to(one, (KY, 128))
    for i, (a, b, q0) in enumerate(KEY_BLOCKS):
        dk = dv = dqt = 0.0
        for h in range(2):
            mine = head_lanes(h)
            s = dg(ka[h, a:b, :], qa[q0:, :], NT)
            p = jnp.exp2(s * C2 + bias[a:b, q0:])
            dp = dg(va[h, a:b, :], ga[q0:, :], NT)
            ds = low(p * dp)
            dv += dg(low(p), jnp.where(mine, g_ref[q0:, :], zero), NN)
            dk += dg(ds, jnp.where(mine, q_ref[q0:, :], zero), NN)
            dqt += dg(ka[h, a:b, :128].T, ds, NN)
        if i == 0:
            dq[...] = dqt
            dk_ref[:256, :] = low(dk[PADP:] * SCALE)
            dv_ref[:256, :] = low(dv[PADP:])
        else:
            dq[:, q0:] += dqt
            dk_ref[q0 : q0 + 256, :] = low(dk * SCALE)
            dv_ref[q0 : q0 + 256, :] = low(dv)
    dq_ref[...] = low(dq[...].T * SCALE)


def attend_backward(qkv, prefix, edges, sums, hidden, ghid, first):
    pairs = qkv.shape[1] // 3 // 128
    width = pairs * 128
    blk = lambda off: pl.BlockSpec((LENGTH, 128), lambda h: (0, off + h))
    pblk = lambda off: pl.BlockSpec((PADP, 128), lambda h: (0, off + first + h))
    return pl.pallas_call(
        backward_kernel,
        grid=(pairs,),
        in_specs=[
            pl.BlockSpec((1, LENGTH), lambda h: (0, 0)),
            pl.BlockSpec((1, KX), lambda h: (0, 0)),
            blk(0), blk(pairs), blk(2 * pairs), pblk(0), pblk(ghid.shape[1] // 128), blk(0), blk(0),
            blk(first),
        ],
        out_specs=[blk(0)] * 3,
        out_shape=[jax.ShapeDtypeStruct((LENGTH, width), jnp.bfloat16)] * 3,
        scratch_shapes=[
            pltpu.VMEM((KY, LENGTH), jnp.float32),
            pltpu.VMEM((LENGTH, 256), jnp.bfloat16),
            pltpu.VMEM((LENGTH, 256), jnp.bfloat16),
            pltpu.VMEM((2, KY, 256), jnp.bfloat16),
            pltpu.VMEM((2, KY, 256), jnp.bfloat16),
            pltpu.VMEM((128, LENGTH), jnp.float32),
        ],
        compiler_params=params(),
    )(*edges, qkv, qkv, qkv, prefix, prefix, sums, hidden, ghid)


def prefix_kernel(
    qa_ref, qb_ref, sa_ref, sb_ref, oa_ref, ob_ref, g_ref, pk_ref, pv_ref,
    total_ref, keys, values, ones, spots, dk_acc, dv_acc,
):
    i = pl.program_id(0)
    heads = keys.shape[0] // PADP
    depth = keys.shape[1]
    half = depth // 2
    col = lax.broadcasted_iota(jnp.int32, (1, depth), 1)

    @pl.when(i == 0)
    def _():
        zero = jnp.bfloat16(0)
        for h in range(heads):
            r = slice(PADP * h, PADP * h + PADP)
            mine = (col >= HEAD * h) & (col < HEAD * h + HEAD)
            keys[r, :] = jnp.where(mine, pk_ref[...], zero)
            values[r, :] = jnp.where(mine, pv_ref[...], zero)
            ones[r, :] = jnp.broadcast_to(low(jnp.where(mine, 1.0, 0.0)), (PADP, depth))
            start = 128 * (h // 2) + 3 * (h % 2)
            spot = (col >= start) & (col < start + 3)
            spots[r, :] = jnp.broadcast_to(low(jnp.where(spot, 1.0, 0.0)), (PADP, depth))
        dk_acc[...] = jnp.zeros_like(dk_acc)
        dv_acc[...] = jnp.zeros_like(dv_acc)

    lane = lax.broadcasted_iota(jnp.int32, (1, PADP * heads), 1)
    g = g_ref[...]
    s = dg(qa_ref[...], keys[:, :half], NT) + dg(qb_ref[...], keys[:, half:], NT)
    s += dg(sa_ref[...], spots[:, :half], NT) + dg(sb_ref[...], spots[:, half:], NT)
    p = jnp.where(lane % PADP < PREFIX, jnp.exp2(s * C2), 0.0)
    dp = dg(g, values[...], NT)
    for c, o_ref in ((0, oa_ref), (half, ob_ref)):
        product = f32(g[:, c : c + half]) * f32(o_ref[...])
        high = low(product)
        dp -= dg(high, ones[:, c : c + half], NT)
        dp -= dg(low(product - f32(high)), ones[:, c : c + half], NT)
    ds = low(p * dp)
    dk_acc[:, :half] += dg(ds, qa_ref[...], TN)
    dk_acc[:, half:] += dg(ds, qb_ref[...], TN)
    dv_acc[...] += dg(low(p), g, TN)

    @pl.when(i == pl.num_programs(0) - 1)
    def _():
        dk = dv = 0.0
        for h in range(heads):
            r = slice(PADP * h, PADP * h + PADP)
            mine = (col >= HEAD * h) & (col < HEAD * h + HEAD)
            dk += jnp.where(mine, dk_acc[r, :], 0.0)
            dv += jnp.where(mine, dv_acc[r, :], 0.0)
        total_ref[:, :depth] = dk * SCALE
        total_ref[:, depth:] = dv


def prefix_call(qkv, sums, hidden, ghid, prefix, block=256):
    rows, depth = ghid.shape
    half = depth // 2
    heads = depth // HEAD
    row = lambda w: pl.BlockSpec((block, w), lambda i: (i, 0))
    whole = lambda c: pl.BlockSpec((PADP, depth), lambda i: (0, c))
    return pl.pallas_call(
        prefix_kernel,
        grid=(rows // block,),
        in_specs=[row(half)] * 6 + [row(depth), whole(0), whole(1)],
        out_specs=pl.BlockSpec((PADP, 2 * depth), lambda i: (0, 0)),
        out_shape=jax.ShapeDtypeStruct((PADP, 2 * depth), jnp.float32),
        scratch_shapes=[pltpu.VMEM((PADP * heads, depth), jnp.bfloat16)] * 4
        + [pltpu.VMEM((PADP * heads, depth), jnp.float32)] * 2,
        compiler_params=params(),
    )(*qkv, *sums, *hidden, ghid, prefix, prefix)


def tree_sum(values):
    while len(values) > 1:
        values = [values[i] + values[i + 1] for i in range(0, len(values), 2)]
    return values[0]


def make_body(dp, fsdp):
    staged = dp == 8 and fsdp == 4

    def body(
        tokens, segments, cotangent, ln1_gain, ln1_bias, w_qkv, b_qkv, w_out, b_out,
        ln2_gain, ln2_bias, w_fc, b_fc, w_proj, b_proj, prefix_embed, w_mid, b_mid, w_kv, b_kv,
    ):
        depth = tokens.shape[1]
        half = depth // 2
        pairs = half // 128
        small = [ln1_gain, ln1_bias, b_out, ln2_gain, ln2_bias, b_proj, b_qkv, b_fc]
        widths = [one.shape[0] for one in small]
        shard_a = jnp.concatenate([w_qkv[:, i * depth : i * depth + half] for i in range(3)], 1)
        shard_b = jnp.concatenate(
            [w_qkv[:, i * depth + half : (i + 1) * depth] for i in range(3)] + [w_out], 1
        )
        if staged:
            order, order_f = place_order(dp, fsdp), direct_order(dp, fsdp)
            za, shard_b = fence(z_stage(shard_a, fsdp), shard_b)
            near, far = glue(*za)
            xa, zb, w_fc, small, segments, prefix_embed, w_proj = fence(
                first_stage(near, far, dp), z_stage(shard_b, fsdp), w_fc, small, segments,
                prefix_embed, w_proj,
            )
            xa, xb = join_stage(xa), glue(*zb)
            xa, xb, small = fence(xa, xb, small)
            ya = second_stage(*xa, dp)
            xb = first_stage(*xb, dp)
            zf = jnp.concatenate([w_fc[None], flip_z(w_fc[None], 2, fsdp)], 0)
            smalls = gather_small(small, dp * fsdp)
            proj = lax.all_gather(w_proj, AXES, axis=0, tiled=True)
        else:
            order = order_f = jnp.arange(PIECES, dtype=jnp.int32)
            smalls = gather_small(small, dp * fsdp)
            pieces_a, pieces_b, pieces_f = (natural_pieces(a) for a in (shard_a, shard_b, w_fc))
            proj = lax.all_gather(w_proj, AXES, axis=0, tiled=True)
        embed_pad = jnp.pad(prefix_embed, ((0, PADP - PREFIX), (0, 0)))
        vectors, bias_a, bias_b, fc_bias = unpack_call(smalls, widths, depth, w_fc.shape[1])
        mid_act, prefix_kv = adapter_call(embed_pad, w_mid, b_mid, w_kv, b_kv)
        edges = segment_edges(segments)
        if staged:
            ready = (order, edges, vectors, bias_a, bias_b, fc_bias, prefix_kv, mid_act)
            ya, xb, zf, ready = fence(ya, xb, zf, ready)
            order, edges, vectors, bias_a, bias_b, fc_bias, prefix_kv, mid_act = ready
            pieces_a = core_stage(ya, dp)
            yb = second_stage(*join_stage(xb), dp)
            far = flip_z(zf, 1, fsdp)
        hidden_a, sums_a, qkv_a, weight_a = front_call(
            order, edges, tokens, vectors, bias_a, prefix_kv, 0, pieces_a
        )
        if staged:
            hidden_a, yb, far = fence(hidden_a, yb, far)
            pieces_b = core_stage(yb, dp)
            own = jnp.concatenate([zf, far], 0)
            near_f = [own] + [flip_dp(own, m, dp) for m in (2, 4, 6)]
            across = flip_dp(own, 1, dp)
        hidden_b, sums_b, qkv_b, weight_b = front_call(
            order, edges, tokens, vectors, bias_b, prefix_kv, pairs, pieces_b
        )
        mixed, normed_two, gact, wout = out_call(
            order, tokens, hidden_a, hidden_b, vectors, cotangent, proj, pieces_b, 3 * half
        )
        if staged:
            mixed, near_f, across = fence(mixed, near_f, across)
            pieces_f = near_f + [across] + [flip_dp(one, 1, dp) for one in near_f[1:]]
        block_out, gmix, ghid = ffn_call(
            order_f, normed_two, gact, fc_bias, proj, mixed, cotangent, vectors, wout, pieces_f
        )
        total = prefix_call(
            (qkv_a, qkv_b), (sums_a, sums_b), (hidden_a, hidden_b), ghid, prefix_kv
        )
        if staged:
            total, ghid = fence(total, ghid)
            spread = [total] + [
                lax.ppermute(total, "fsdp", [(i, i ^ m) for i in range(fsdp)]) for m in (1, 2, 3)
            ]
        gqa, gka, gva = attend_backward(qkv_a, prefix_kv, edges, sums_a, hidden_a, ghid, 0)
        if staged:
            gqa, spread, ghid = fence(gqa, spread, ghid)
            total = tree_sum(spread)
            total, ghid = fence(total, ghid)
            spread = [total] + [flip_dp(total, m, dp) for m in (1, 2, 3)]
        gqb, gkb, gvb = attend_backward(qkv_b, prefix_kv, edges, sums_b, hidden_b, ghid, pairs)
        if staged:
            gqb, spread = fence(gqb, spread)
            total = tree_sum(spread)
            gqb, total = fence(gqb, total)
            other = flip_dp(total, 4, dp)
        else:
            total = lax.psum(total, AXES)
            other = jnp.zeros_like(total)
        grad_tokens = final_call(
            tokens, gmix, vectors, weight_a, weight_b, (gqa, gka, gva, gqb, gkb, gvb)
        )
        adapter = adapter_back_call(total, other, embed_pad, w_mid, w_kv, mid_act)
        return (block_out, grad_tokens) + adapter

    return body


def solution(mesh):
    dp, fsdp = mesh.shape["dp"], mesh.shape["fsdp"]
    rows, flat = P(AXES, None), P(AXES)
    return jax.shard_map(
        make_body(dp, fsdp),
        mesh=mesh,
        in_specs=(
            rows, flat, rows, flat, flat, rows, flat, rows, flat, flat, flat, rows, flat, rows,
            flat, P(), P(), P(), P(), P(),
        ),
        out_specs=(rows, rows, P(), P(), P(), P(), P()),
        check_vma=False,
    )
```

```python
import jax
import jax.numpy as jnp
from jax import lax
from jax.experimental import pallas as pl
from jax.experimental.pallas import tpu as pltpu
from jax.sharding import PartitionSpec as P

HEAD = 64
PREFIX = 10
PADP = 16
LENGTH = 1024
AXES = ("dp", "fsdp")
LOG2E = 1.4426950408889634
SCALE = HEAD**-0.5
C2 = SCALE * LOG2E
NEG = -1e30
KX = 1152
KY = PADP + LENGTH
NT = (((1,), (1,)), ((), ()))
NN = (((1,), (0,)), ((), ()))
TN = (((0,), (0,)), ((), ()))
PIECES = 32
MB = 1024 * 1024


def dg(left, right, dims):
    return lax.dot_general(left, right, dims, preferred_element_type=jnp.float32)


def f32(value):
    return value.astype(jnp.float32)


def low(value):
    return value.astype(jnp.bfloat16)


def params():
    return pltpu.CompilerParams(vmem_limit_bytes=60 * MB)


def flip_dp(value, mask, size):
    return lax.ppermute(value, "dp", [(i, i ^ mask) for i in range(size)])


def flip_z(value, mask, size):
    return lax.ppermute(value, "fsdp", [(i, i ^ mask) for i in range(size)])


def fence(*values):
    return lax.optimization_barrier(values)


def z_stage(shard, fsdp):
    own = shard[None]
    return [own] + [flip_z(own, m, fsdp) for m in (2, 1, 3)]


def first_stage(near, far, dp):
    return near, far, flip_dp(near, 2, dp), flip_dp(far, 4, dp)


def direct_order(dp, fsdp):
    d = lax.axis_index("dp")
    z = lax.axis_index("fsdp")
    places = []
    for core in (0, 1):
        for mask in (0, 2, 4, 6):
            places += [(d ^ (core ^ mask)) * fsdp + (z ^ turn) for turn in (0, 2, 1, 3)]
    return jnp.stack(places).astype(jnp.int32)


def glue_kernel(a_ref, b_ref, c_ref, d_ref, near_ref, far_ref):
    size = a_ref.shape[0]
    near_ref[:size] = a_ref[...]
    near_ref[size:] = b_ref[...]
    far_ref[:size] = c_ref[...]
    far_ref[size:] = d_ref[...]


def glue(a, b, c, d):
    vmem = pl.BlockSpec(memory_space=pltpu.VMEM)
    shape = (2 * a.shape[0],) + a.shape[1:]
    return pl.pallas_call(
        glue_kernel,
        in_specs=[vmem] * 4,
        out_specs=[vmem] * 2,
        out_shape=[jax.ShapeDtypeStruct(shape, a.dtype)] * 2,
    )(a, b, c, d)


def join_stage(state):
    return glue(state[0], state[2], state[1], state[3])


def second_stage(near, far, dp):
    return [near, flip_dp(near, 4, dp), far, flip_dp(far, 2, dp)]


def core_stage(plane, dp):
    return plane + [flip_dp(one, 1, dp) for one in plane]


def place_order(dp, fsdp):
    d = lax.axis_index("dp")
    z = lax.axis_index("fsdp")
    places = []
    for core in (0, 1):
        for first, second, base in ((2, 4, 0), (4, 2, 1)):
            for outer in (0, second):
                for inner in (0, first):
                    for turn in (base, base ^ 2):
                        places.append((d ^ (core ^ outer ^ inner)) * fsdp + (z ^ turn))
    return jnp.stack(places).astype(jnp.int32)


SMALL = 8


def pack_kernel(*refs):
    ins, out_ref = refs[:SMALL], refs[SMALL]
    row = jnp.zeros((SMALL, 128), jnp.float32)
    spot = lax.broadcasted_iota(jnp.int32, (SMALL, 128), 0)
    for i, one in enumerate(ins):
        wide = one.shape[1]
        value = f32(one[...])
        if wide < 128:
            value = jnp.concatenate([value, jnp.zeros((1, 128 - wide), jnp.float32)], 1)
        row = jnp.where(spot == i, value, row)
    out_ref[...] = jnp.broadcast_to(low(row)[None], out_ref.shape)


def pack_call(small, devices):
    vmem = pl.BlockSpec(memory_space=pltpu.VMEM)
    return pl.pallas_call(
        pack_kernel,
        in_specs=[vmem] * SMALL,
        out_specs=vmem,
        out_shape=jax.ShapeDtypeStruct((devices, SMALL, 128), jnp.bfloat16),
    )(*[one[None] for one in small])


def unpack_kernel(widths, all_ref, rows_ref, qa_ref, qb_ref, fc_ref):
    devices = all_ref.shape[0]
    depth = rows_ref.shape[1]
    half = depth // 2

    def spread(i, place):
        share = all_ref[:, i, :]
        lane = lax.broadcasted_iota(jnp.int32, (128, place.shape[1]), 0)
        pick = low(jnp.where(lane == place % widths[i], 1.0, 0.0))
        owner = lax.broadcasted_iota(jnp.int32, (devices, place.shape[1]), 0)
        found = jnp.where(owner == place // widths[i], dg(share, pick, NN), 0.0)
        return jnp.sum(found, axis=0, keepdims=True)

    natural = lax.broadcasted_iota(jnp.int32, (1, depth), 1)
    for i in range(SMALL - 2):
        rows_ref[i : i + 1, :] = spread(i, natural)
    rows_ref[SMALL - 2 :, :] = jnp.zeros((2, depth), jnp.float32)
    short = lax.broadcasted_iota(jnp.int32, (1, half), 1)
    for k in range(3):
        qa_ref[:, k * half : (k + 1) * half] = spread(SMALL - 2, short + k * depth)
        qb_ref[:, k * half : (k + 1) * half] = spread(SMALL - 2, short + k * depth + half)
    for k in range(fc_ref.shape[1] // depth):
        fc_ref[:, k * depth : (k + 1) * depth] = spread(SMALL - 1, natural + k * depth)


def unpack_call(gathered, widths, depth, wide):
    vmem = pl.BlockSpec(memory_space=pltpu.VMEM)
    shapes = ((SMALL, depth), (1, 3 * depth // 2), (1, 3 * depth // 2), (1, wide))
    return pl.pallas_call(
        lambda *refs: unpack_kernel(widths, *refs),
        in_specs=[vmem],
        out_specs=[vmem] * 4,
        out_shape=[jax.ShapeDtypeStruct(shape, jnp.float32) for shape in shapes],
    )(gathered)


def adapter_kernel(embed_ref, wm_ref, bm_ref, wkv_ref, bkv_ref, mid_ref, kv_ref):
    mid = jnp.tanh(dg(embed_ref[...], wm_ref[...], NN) + f32(bm_ref[...]))
    mid_ref[...] = mid
    kv = low(dg(low(mid), wkv_ref[...], NN) + f32(bkv_ref[...]))
    row = lax.broadcasted_iota(jnp.int32, kv.shape, 0)
    kv_ref[...] = jnp.where(row < PREFIX, kv, jnp.bfloat16(0))


def adapter_call(embed, w_mid, b_mid, w_kv, b_kv):
    vmem = pl.BlockSpec(memory_space=pltpu.VMEM)
    return pl.pallas_call(
        adapter_kernel,
        in_specs=[vmem] * 5,
        out_specs=[vmem] * 2,
        out_shape=[
            jax.ShapeDtypeStruct((PADP, w_mid.shape[1]), jnp.float32),
            jax.ShapeDtypeStruct((PADP, w_kv.shape[1]), jnp.bfloat16),
        ],
    )(embed, w_mid, b_mid[None], w_kv, b_kv[None])


def adapter_back_kernel(
    own_ref, other_ref, embed_ref, wm_ref, wkv_ref, mid_ref, ge_ref, gmw_ref, gmb_ref, gkw_ref, gkb_ref
):
    low_sum = low(own_ref[...] + other_ref[...])
    mid = mid_ref[...]
    gkw_ref[...] = dg(low(mid), low_sum, TN)
    gkb_ref[...] = jnp.sum(f32(low_sum), axis=0, keepdims=True)
    grad = low(dg(low_sum, wkv_ref[...], NT) * (1.0 - mid * mid))
    gmw_ref[...] = dg(embed_ref[...], grad, TN)
    gmb_ref[...] = jnp.sum(f32(grad), axis=0, keepdims=True)
    ge_ref[...] = dg(grad, wm_ref[...], NT)[:PREFIX]


def adapter_back_call(own, other, embed, w_mid, w_kv, mid):
    vmem = pl.BlockSpec(memory_space=pltpu.VMEM)
    depth, middle = w_mid.shape
    shapes = ((PREFIX, depth), (depth, middle), (1, middle), w_kv.shape, (1, w_kv.shape[1]))
    found = pl.pallas_call(
        adapter_back_kernel,
        in_specs=[vmem] * 6,
        out_specs=[vmem] * 5,
        out_shape=[jax.ShapeDtypeStruct(shape, jnp.float32) for shape in shapes],
    )(own, other, embed, w_mid, w_kv, mid)
    return found[0], found[1], found[2][0], found[3], found[4][0]


def gather_small(small, devices):
    return lax.all_to_all(pack_call(small, devices), AXES, 0, 0, tiled=True)


def natural_pieces(shard):
    whole = lax.all_gather(shard, AXES, axis=0, tiled=True)
    whole = whole.reshape(8, 4, whole.shape[0] // PIECES, *whole.shape[1:])
    return [whole[i] for i in range(8)]


def place_pieces(order_ref, piece_refs, target_ref, columns, sems):
    copies = []
    for b in range(8):
        for k in range(4):
            i = b * 4 + k
            row = pl.multiple_of(order_ref[i] * PIECES, PIECES)
            copies.append(
                pltpu.make_async_copy(
                    piece_refs[b].at[k, :, columns],
                    target_ref.at[pl.ds(row, PIECES), :],
                    sems.at[i],
                )
            )
    return copies


def anyspec():
    return pl.BlockSpec(memory_space=pl.ANY)


def smem():
    return pl.BlockSpec(memory_space=pltpu.SMEM)


def norm_rows(values):
    mean = jnp.mean(values, axis=-1, keepdims=True)
    centred = values - mean
    spread = jnp.mean(centred * centred, axis=-1, keepdims=True)
    return centred * lax.rsqrt(spread + 1e-05), spread


def norm_pull(values, gain_row, grad):
    unit, spread = norm_rows(values)
    weighted = grad * gain_row
    first = jnp.mean(weighted, axis=-1, keepdims=True)
    second = jnp.mean(weighted * unit, axis=-1, keepdims=True)
    return (weighted - first - unit * second) * lax.rsqrt(spread + 1e-05)


HIDDEN = 512


def out_kernel(
    column, order_ref, tokens_ref, ha_ref, hb_ref, vec_ref, cot_ref, proj_ref, *rest
):
    pieces, (mixed_ref, normed_ref, gact_ref, weight_ref, sems) = rest[:8], rest[8:]

    def copies():
        width = weight_ref.shape[1]
        return place_pieces(order_ref, pieces, weight_ref, pl.ds(column, width), sems)

    @pl.when(pl.program_id(0) == 0)
    def _():
        for one in copies():
            one.start()

    for k in range(gact_ref.shape[0]):
        rows = proj_ref[k * HIDDEN : (k + 1) * HIDDEN, :]
        gact_ref[k] = low(dg(cot_ref[...], rows, NT))

    @pl.when(pl.program_id(0) == 0)
    def _():
        for one in copies():
            one.wait()

    half = ha_ref.shape[1]
    mixed = f32(tokens_ref[...]) + vec_ref[2:3, :]
    mixed += dg(ha_ref[...], weight_ref[:half, :], NN)
    mixed += dg(hb_ref[...], weight_ref[half:, :], NN)
    mixed_ref[...] = mixed
    unit, _ = norm_rows(mixed)
    normed_ref[...] = low(unit * vec_ref[3:4, :] + vec_ref[4:5, :])


def out_call(order, tokens, hidden_a, hidden_b, vectors, cot, proj, pieces, column):
    rows, depth = tokens.shape
    blocks = proj.shape[0] // HIDDEN
    steps = blocks // 2
    row = lambda w: pl.BlockSpec((rows // steps, w), lambda j: (j, 0))
    whole = lambda s: pl.BlockSpec(s, lambda j: (0, 0))
    return pl.pallas_call(
        lambda *refs: out_kernel(column, *refs),
        grid=(steps,),
        in_specs=[smem(), row(depth), row(depth // 2), row(depth // 2), whole(vectors.shape)]
        + [whole(cot.shape), pl.BlockSpec((2 * HIDDEN, depth), lambda j: (j, 0))]
        + [anyspec()] * 8,
        out_specs=[
            row(depth),
            row(depth),
            pl.BlockSpec((2, rows, HIDDEN), lambda j: (j, 0, 0)),
            whole((depth, depth)),
        ],
        out_shape=[
            jax.ShapeDtypeStruct((rows, depth), jnp.float32),
            jax.ShapeDtypeStruct((rows, depth), jnp.bfloat16),
            jax.ShapeDtypeStruct((blocks, rows, HIDDEN), jnp.bfloat16),
            jax.ShapeDtypeStruct((depth, depth), jnp.bfloat16),
        ],
        scratch_shapes=[pltpu.SemaphoreType.DMA((PIECES,))],
        compiler_params=params(),
    )(order, tokens, hidden_a, hidden_b, vectors, cot, proj, *pieces)


GELU_A = 0.7978845608028654
GELU_B = 0.044715


def gelu_pair(value):
    square = value * value
    half = 0.5 + 0.5 * jnp.tanh(value * (GELU_A + GELU_A * GELU_B * square))
    act = value * half
    slope = half + 2.0 * act * (1.0 - half) * (GELU_A + 3.0 * GELU_A * GELU_B * square)
    return act, slope


def ffn_kernel(
    order_ref, bias_ref, vec_ref, normed_hbm, gact_hbm, proj_hbm, mixed_hbm, cot_hbm, wout_hbm, *rest
):
    pieces, (block_hbm, gmix_hbm, ghid_hbm) = rest[:8], rest[8:11]
    normed, gact, fc, proj, pre, act, gpre, acc_ref, gacc_ref = rest[11:20]
    nsem, gsem, psem, fsem, tsem, osem = rest[20:]
    blocks = gact.shape[0]
    wide = blocks * HIDDEN // 2

    def columns(half):
        found = []
        for p in range(PIECES):
            row = pl.multiple_of(order_ref[p] * PIECES, PIECES)
            source = pieces[p // 4].at[p % 4, :, pl.ds(half * wide, wide)]
            target = fc.at[pl.ds(row, PIECES), pl.ds(half * wide, wide)]
            found.append(pltpu.make_async_copy(source, target, fsem.at[half, p]))
        return found

    def gact_copy(j):
        return pltpu.make_async_copy(gact_hbm.at[j], gact.at[j], gsem.at[j])

    def proj_copy(j):
        rows = pl.ds(pl.multiple_of(j * HIDDEN, HIDDEN), HIDDEN)
        return pltpu.make_async_copy(proj_hbm.at[rows, :], proj.at[rows, :], psem.at[j])

    def step(j, slot, first, second, third):
        if first:
            c = pl.ds(pl.multiple_of(j * HIDDEN, HIDDEN), HIDDEN)
            pre[slot] = dg(normed[...], fc[:, c], NN) + bias_ref[:, c]
        if second:
            value, slope = gelu_pair(pre[1 - slot])
            act[1 - slot] = low(value)
            gpre[1 - slot] = low(f32(gact[j - 1]) * slope)
        if third:
            c = pl.ds(pl.multiple_of((j - 2) * HIDDEN, HIDDEN), HIDDEN)
            acc_ref[...] += dg(act[slot], proj[c, :], NN)
            gacc_ref[...] += dg(gpre[slot], fc[:, c], NT)

    start = pltpu.make_async_copy(normed_hbm, normed, nsem)
    start.start()
    for one in columns(0):
        one.start()
    early = [gact_copy(1), gact_copy(2), proj_copy(0), proj_copy(1)]
    later = columns(1) + [gact_copy(j) for j in range(3, blocks)]
    later += [proj_copy(j) for j in range(2, blocks)]
    for one in [gact_copy(0)] + early + later:
        one.start()
    acc_ref[...] = jnp.zeros_like(acc_ref)
    gacc_ref[...] = jnp.zeros_like(gacc_ref)
    start.wait()
    for one in columns(0):
        one.wait()
    step(0, 0, True, False, False)
    gact_copy(0).wait()
    step(1, 1, True, True, False)
    for one in early:
        one.wait()
    step(2, 0, True, True, True)
    step(3, 1, True, True, True)
    for one in later:
        one.wait()

    def pair(k, carry):
        for i in (0, 1):
            step(2 * k + 2 + i, i, True, True, True)
        return carry

    lax.fori_loop(1, blocks // 2 - 1, pair, 0)
    sides = [pl.ds(k * HIDDEN, HIDDEN) for k in (0, 1)]
    late = [pltpu.make_async_copy(cot_hbm, normed, tsem.at[0])]
    for k, c in enumerate(sides):
        late.append(pltpu.make_async_copy(wout_hbm.at[:, c], gact.at[k], tsem.at[1 + k]))
    for one in late:
        one.start()
    step(blocks, 0, False, True, True)
    for k, c in enumerate(sides):
        late.append(pltpu.make_async_copy(mixed_hbm.at[:, c], pre.at[k], tsem.at[3 + k]))
        late[-1].start()
    step(blocks + 1, 1, False, False, True)
    for one in late:
        one.wait()
    outs = []
    size = normed.shape[0] // 4
    for i in range(4):
        r = slice(i * size, (i + 1) * size)
        value = jnp.concatenate([pre[0, r, :], pre[1, r, :]], 1)
        block = low(value + acc_ref[r, :] + vec_ref[5:6, :])
        gmix = f32(normed[r, :]) + norm_pull(value, vec_ref[3:4, :], gacc_ref[r, :])
        gmix_low = low(gmix)
        ghid = dg(gmix_low[:, :HIDDEN], gact[0], NT) + dg(gmix_low[:, HIDDEN:], gact[1], NT)
        for k, c in enumerate((slice(0, HIDDEN), slice(HIDDEN, 2 * HIDDEN))):
            act[k, r, :] = block[:, c]
            pre[k, r, :] = gmix[:, c]
            gpre[k, r, :] = low(ghid[:, c])
            for m, (source, target) in enumerate(
                ((act, block_hbm), (pre, gmix_hbm), (gpre, ghid_hbm))
            ):
                spot = target.at[r, sides[k]]
                copy = pltpu.make_async_copy(source.at[k, r, :], spot, osem.at[i, k, m])
                copy.start()
                outs.append(copy)
    for one in outs:
        one.wait()


def ffn_call(order, normed, gact, bias, proj, mixed, cot, vectors, wout, pieces):
    rows, depth = normed.shape
    blocks = gact.shape[0]
    wide = blocks * HIDDEN
    vmem = pl.BlockSpec(memory_space=pltpu.VMEM)
    return pl.pallas_call(
        ffn_kernel,
        in_specs=[smem(), vmem, vmem] + [anyspec()] * 14,
        out_specs=[anyspec()] * 3,
        out_shape=[
            jax.ShapeDtypeStruct((rows, depth), jnp.bfloat16),
            jax.ShapeDtypeStruct((rows, depth), jnp.float32),
            jax.ShapeDtypeStruct((rows, depth), jnp.bfloat16),
        ],
        scratch_shapes=[
            pltpu.VMEM((rows, depth), jnp.bfloat16),
            pltpu.VMEM(gact.shape, jnp.bfloat16),
            pltpu.VMEM((depth, wide), jnp.bfloat16),
            pltpu.VMEM((wide, depth), jnp.bfloat16),
            pltpu.VMEM((2, rows, HIDDEN), jnp.float32),
            pltpu.VMEM((2, rows, HIDDEN), jnp.bfloat16),
            pltpu.VMEM((2, rows, HIDDEN), jnp.bfloat16),
            pltpu.VMEM((rows, depth), jnp.float32),
            pltpu.VMEM((rows, depth), jnp.float32),
            pltpu.SemaphoreType.DMA,
            pltpu.SemaphoreType.DMA((blocks,)),
            pltpu.SemaphoreType.DMA((blocks,)),
            pltpu.SemaphoreType.DMA((2, PIECES)),
            pltpu.SemaphoreType.DMA((5,)),
            pltpu.SemaphoreType.DMA((4, 2, 3)),
        ],
        compiler_params=params(),
    )(order, bias, vectors, normed, gact, proj, mixed, cot, wout, *pieces)


def final_kernel(tokens_ref, gmix_ref, vec_ref, wa_ref, wb_ref, *rest):
    grads, out_ref = rest[:6], rest[6]
    total = None
    for i in range(6):
        half = grads[i].shape[1]
        c = (i % 3) * half
        weight = (wa_ref if i < 3 else wb_ref)[:, c : c + half]
        part = dg(grads[i][...], weight, NT)
        total = part if total is None else total + part
    pulled = norm_pull(f32(tokens_ref[...]), vec_ref[0:1, :], total)
    out_ref[...] = low(gmix_ref[...] + pulled)


def final_call(tokens, gmix, vectors, wa, wb, grads, block=256):
    rows, depth = tokens.shape
    row = lambda w: pl.BlockSpec((block, w), lambda i: (i, 0))
    whole = lambda s: pl.BlockSpec(s, lambda i: (0, 0))
    return pl.pallas_call(
        final_kernel,
        grid=(rows // block,),
        in_specs=[row(depth), row(depth), whole(vectors.shape), whole(wa.shape), whole(wb.shape)]
        + [row(grads[0].shape[1])] * 6,
        out_specs=row(depth),
        out_shape=jax.ShapeDtypeStruct((rows, depth), jnp.bfloat16),
        compiler_params=params(),
    )(tokens, gmix, vectors, wa, wb, *grads)


def split3(value):
    high = f32(low(value))
    rest = value - high
    middle = f32(low(rest))
    return high, middle, rest - middle


QUERY_BLOCKS = ((0, 240, 256), (240, 496, 512), (496, 752, 768), (752, 1024, 1152))
KEY_BLOCKS = ((0, 272, 0), (272, 528, 256), (528, 784, 512), (784, 1040, 768))


def lane_pieces(value):
    lane = lax.broadcasted_iota(jnp.int32, (1, 128), 1)
    high, middle, rest = split3(value)
    picked = jnp.where(lane % 3 == 0, high, jnp.where(lane % 3 == 1, middle, rest))
    return low(jnp.where(lane < 6, picked, 0.0))


def head_spots():
    row = lax.broadcasted_iota(jnp.int32, (128, 128), 0)
    col = lax.broadcasted_iota(jnp.int32, (128, 128), 1)
    return low(jnp.where((row // HEAD == col // 3) & (col < 6), 1.0, 0.0))


def as_column(row):
    return jnp.broadcast_to(f32(row), (8, row.shape[1])).T[:, 0:1].astype(jnp.int32)


def head_lanes(h):
    lane = lax.broadcasted_iota(jnp.int32, (1, 128), 1)
    return (lane >= HEAD * h) & (lane < HEAD * h + HEAD)


def front_kernel(
    order_ref, seg_ref, keys_ref, tokens_ref, vec_ref, qb_ref, pk_ref, pv_ref, *rest
):
    pieces, (o_ref, l_ref, qkv_ref, weight_ref, bias, kx, vx, normed, sems) = rest[:8], rest[8:]
    step = pl.program_id(0)
    width = weight_ref.shape[1]

    @pl.when(step == 0)
    def _():
        copies = place_pieces(order_ref, pieces, weight_ref, pl.ds(0, width), sems)
        for one in copies:
            one.start()
        row = lax.broadcasted_iota(jnp.int32, (LENGTH, KX), 0) + PADP
        col = lax.broadcasted_iota(jnp.int32, (LENGTH, KX), 1)
        seen = ((as_column(seg_ref[...]) == keys_ref[...]) & (col <= row)) | (col < PREFIX)
        bias[...] = jnp.where(seen, 0.0, NEG)
        unit, _ = norm_rows(f32(tokens_ref[...]))
        normed[...] = low(unit * vec_ref[0:1, :] + vec_ref[1:2, :])
        kx[...] = jnp.zeros_like(kx)
        vx[...] = jnp.zeros_like(vx)
        for h in range(2):
            vx[h, :, 128:] = jnp.ones((KX, 128), jnp.bfloat16)
        for one in copies:
            one.wait()
        for c in range(0, width, 512):
            part = dg(normed[...], weight_ref[:, c : c + 512], NN) + qb_ref[:, c : c + 512]
            qkv_ref[:, c : c + 512] = low(part)

    lane = lax.broadcasted_iota(jnp.int32, (1, 128), 1)
    zero = jnp.bfloat16(0)
    at = [pl.ds(pl.multiple_of(i * (width // 3) + step * 128, 128), 128) for i in range(3)]
    for h in range(2):
        mine = head_lanes(h)
        kx[h, :PADP, :] = jnp.where(mine, pk_ref[...], zero)
        kx[h, PADP:KY, :] = jnp.where(mine, qkv_ref[:, at[1]], zero)
        vx[h, :PADP, :128] = jnp.where(mine, pv_ref[...], zero)
        vx[h, PADP:KY, :128] = jnp.where(mine, qkv_ref[:, at[2]], zero)
    for a, b, nk in QUERY_BLOCKS:
        outs, sums = [], []
        for h in range(2):
            s = dg(qkv_ref[a:b, at[0]], kx[h, :nk, :], NT) * C2 + bias[a:b, :nk]
            top = jnp.max(s, axis=1, keepdims=True)
            o = dg(low(jnp.exp2(s - top)), vx[h, :nk, :], NN)
            mass = o[:, 128:]
            outs.append(o[:, :128] / mass)
            sums.append((top + jnp.log2(mass)) * (-1.0 / C2))
        o_ref[a:b, :] = low(outs[0] + outs[1])
        aug = 0.0
        for i, part in enumerate(split3(sums[0]) + split3(sums[1])):
            aug = jnp.where(lane == i, part, aug)
        l_ref[a:b, :] = low(aug)


def segment_edges(segments):
    keys = jnp.pad(segments, (PADP, KX - KY), constant_values=-1)
    return segments[None, :], keys[None, :]


def front_call(order, edges, tokens, vectors, qkv_bias, prefix, first, pieces):
    depth = tokens.shape[1]
    width = qkv_bias.shape[1]
    pairs = width // 3 // 128
    whole = lambda s: pl.BlockSpec(s, lambda h: (0, 0), pipeline_mode=pl.Buffered(1))
    blk = pl.BlockSpec((LENGTH, 128), lambda h: (0, h))
    pblk = lambda off: pl.BlockSpec((PADP, 128), lambda h: (0, off + first + h))
    return pl.pallas_call(
        front_kernel,
        grid=(pairs,),
        in_specs=[smem(), whole((1, LENGTH)), whole((1, KX)), whole(tokens.shape)]
        + [whole(vectors.shape), whole(qkv_bias.shape), pblk(0), pblk(depth // 128)]
        + [anyspec()] * 8,
        out_specs=[blk, blk, whole((LENGTH, width)), whole((depth, width))],
        out_shape=[jax.ShapeDtypeStruct((LENGTH, width // 3), jnp.bfloat16)] * 2
        + [
            jax.ShapeDtypeStruct((LENGTH, width), jnp.bfloat16),
            jax.ShapeDtypeStruct((depth, width), jnp.bfloat16),
        ],
        scratch_shapes=[
            pltpu.VMEM((LENGTH, KX), jnp.float32),
            pltpu.VMEM((2, KX, 128), jnp.bfloat16),
            pltpu.VMEM((2, KX, 256), jnp.bfloat16),
            pltpu.VMEM(tokens.shape, jnp.bfloat16),
            pltpu.SemaphoreType.DMA((PIECES,)),
        ],
        compiler_params=params(),
    )(order, *edges, tokens, vectors, qkv_bias, prefix, prefix, *pieces)


def backward_kernel(
    seg_ref, keys_ref, q_ref, k_ref, v_ref, pk_ref, pv_ref, l_ref, o_ref, g_ref,
    dq_ref, dk_ref, dv_ref, bias, qa, ga, ka, va, dq,
):
    @pl.when(pl.program_id(0) == 0)
    def _():
        row = lax.broadcasted_iota(jnp.int32, (KY, LENGTH), 0)
        col = lax.broadcasted_iota(jnp.int32, (KY, LENGTH), 1) + PADP
        keys = as_column(keys_ref[...])[:KY]
        seen = ((keys == seg_ref[...]) & (row <= col)) | (row < PREFIX)
        bias[...] = jnp.where(seen, 0.0, NEG)

    lane = lax.broadcasted_iota(jnp.int32, (1, 128), 1)
    zero = jnp.bfloat16(0)
    qa[:, :128] = q_ref[...]
    qa[:, 128:] = l_ref[...]
    ga[:, :128] = g_ref[...]
    product = f32(g_ref[...]) * f32(o_ref[...])
    high = low(product)
    spots = head_spots()
    inner = dg(high, spots, NN) + dg(low(product - f32(high)), spots, NN)
    ga[:, 128:] = lane_pieces(-inner)
    for h in range(2):
        mine = head_lanes(h)
        one = low(jnp.where((lane >= 3 * h) & (lane < 3 * h + 3), 1.0, 0.0))
        ka[h, :PADP, :128] = jnp.where(mine, pk_ref[...], zero)
        ka[h, PADP:, :128] = jnp.where(mine, k_ref[...], zero)
        va[h, :PADP, :128] = jnp.where(mine, pv_ref[...], zero)
        va[h, PADP:, :128] = jnp.where(mine, v_ref[...], zero)
        ka[h, :, 128:] = jnp.broadcast_to(one, (KY, 128))
        va[h, :, 128:] = jnp.broadcast_to(one, (KY, 128))
    for i, (a, b, q0) in enumerate(KEY_BLOCKS):
        dk = dv = dqt = 0.0
        for h in range(2):
            mine = head_lanes(h)
            s = dg(ka[h, a:b, :], qa[q0:, :], NT)
            p = jnp.exp2(s * C2 + bias[a:b, q0:])
            dp = dg(va[h, a:b, :], ga[q0:, :], NT)
            ds = low(p * dp)
            dv += dg(low(p), jnp.where(mine, g_ref[q0:, :], zero), NN)
            dk += dg(ds, jnp.where(mine, q_ref[q0:, :], zero), NN)
            dqt += dg(ka[h, a:b, :128].T, ds, NN)
        if i == 0:
            dq[...] = dqt
            dk_ref[:256, :] = low(dk[PADP:] * SCALE)
            dv_ref[:256, :] = low(dv[PADP:])
        else:
            dq[:, q0:] += dqt
            dk_ref[q0 : q0 + 256, :] = low(dk * SCALE)
            dv_ref[q0 : q0 + 256, :] = low(dv)
    dq_ref[...] = low(dq[...].T * SCALE)


def attend_backward(qkv, prefix, edges, sums, hidden, ghid, first):
    pairs = qkv.shape[1] // 3 // 128
    width = pairs * 128
    blk = lambda off: pl.BlockSpec((LENGTH, 128), lambda h: (0, off + h))
    pblk = lambda off: pl.BlockSpec((PADP, 128), lambda h: (0, off + first + h))
    return pl.pallas_call(
        backward_kernel,
        grid=(pairs,),
        in_specs=[
            pl.BlockSpec((1, LENGTH), lambda h: (0, 0)),
            pl.BlockSpec((1, KX), lambda h: (0, 0)),
            blk(0), blk(pairs), blk(2 * pairs), pblk(0), pblk(ghid.shape[1] // 128), blk(0), blk(0),
            blk(first),
        ],
        out_specs=[blk(0)] * 3,
        out_shape=[jax.ShapeDtypeStruct((LENGTH, width), jnp.bfloat16)] * 3,
        scratch_shapes=[
            pltpu.VMEM((KY, LENGTH), jnp.float32),
            pltpu.VMEM((LENGTH, 256), jnp.bfloat16),
            pltpu.VMEM((LENGTH, 256), jnp.bfloat16),
            pltpu.VMEM((2, KY, 256), jnp.bfloat16),
            pltpu.VMEM((2, KY, 256), jnp.bfloat16),
            pltpu.VMEM((128, LENGTH), jnp.float32),
        ],
        compiler_params=params(),
    )(*edges, qkv, qkv, qkv, prefix, prefix, sums, hidden, ghid)


def prefix_kernel(
    qa_ref, qb_ref, sa_ref, sb_ref, oa_ref, ob_ref, g_ref, pk_ref, pv_ref,
    total_ref, keys, values, ones, spots, dk_acc, dv_acc,
):
    i = pl.program_id(0)
    heads = keys.shape[0] // PADP
    depth = keys.shape[1]
    half = depth // 2
    col = lax.broadcasted_iota(jnp.int32, (1, depth), 1)

    @pl.when(i == 0)
    def _():
        zero = jnp.bfloat16(0)
        for h in range(heads):
            r = slice(PADP * h, PADP * h + PADP)
            mine = (col >= HEAD * h) & (col < HEAD * h + HEAD)
            keys[r, :] = jnp.where(mine, pk_ref[...], zero)
            values[r, :] = jnp.where(mine, pv_ref[...], zero)
            ones[r, :] = jnp.broadcast_to(low(jnp.where(mine, 1.0, 0.0)), (PADP, depth))
            start = 128 * (h // 2) + 3 * (h % 2)
            spot = (col >= start) & (col < start + 3)
            spots[r, :] = jnp.broadcast_to(low(jnp.where(spot, 1.0, 0.0)), (PADP, depth))
        dk_acc[...] = jnp.zeros_like(dk_acc)
        dv_acc[...] = jnp.zeros_like(dv_acc)

    lane = lax.broadcasted_iota(jnp.int32, (1, PADP * heads), 1)
    g = g_ref[...]
    s = dg(qa_ref[...], keys[:, :half], NT) + dg(qb_ref[...], keys[:, half:], NT)
    s += dg(sa_ref[...], spots[:, :half], NT) + dg(sb_ref[...], spots[:, half:], NT)
    p = jnp.where(lane % PADP < PREFIX, jnp.exp2(s * C2), 0.0)
    dp = dg(g, values[...], NT)
    for c, o_ref in ((0, oa_ref), (half, ob_ref)):
        product = f32(g[:, c : c + half]) * f32(o_ref[...])
        high = low(product)
        dp -= dg(high, ones[:, c : c + half], NT)
        dp -= dg(low(product - f32(high)), ones[:, c : c + half], NT)
    ds = low(p * dp)
    dk_acc[:, :half] += dg(ds, qa_ref[...], TN)
    dk_acc[:, half:] += dg(ds, qb_ref[...], TN)
    dv_acc[...] += dg(low(p), g, TN)

    @pl.when(i == pl.num_programs(0) - 1)
    def _():
        dk = dv = 0.0
        for h in range(heads):
            r = slice(PADP * h, PADP * h + PADP)
            mine = (col >= HEAD * h) & (col < HEAD * h + HEAD)
            dk += jnp.where(mine, dk_acc[r, :], 0.0)
            dv += jnp.where(mine, dv_acc[r, :], 0.0)
        total_ref[:, :depth] = dk * SCALE
        total_ref[:, depth:] = dv


def prefix_call(qkv, sums, hidden, ghid, prefix, block=256):
    rows, depth = ghid.shape
    half = depth // 2
    heads = depth // HEAD
    row = lambda w: pl.BlockSpec((block, w), lambda i: (i, 0))
    whole = lambda c: pl.BlockSpec((PADP, depth), lambda i: (0, c))
    return pl.pallas_call(
        prefix_kernel,
        grid=(rows // block,),
        in_specs=[row(half)] * 6 + [row(depth), whole(0), whole(1)],
        out_specs=pl.BlockSpec((PADP, 2 * depth), lambda i: (0, 0)),
        out_shape=jax.ShapeDtypeStruct((PADP, 2 * depth), jnp.float32),
        scratch_shapes=[pltpu.VMEM((PADP * heads, depth), jnp.bfloat16)] * 4
        + [pltpu.VMEM((PADP * heads, depth), jnp.float32)] * 2,
        compiler_params=params(),
    )(*qkv, *sums, *hidden, ghid, prefix, prefix)


def tree_sum(values):
    while len(values) > 1:
        values = [values[i] + values[i + 1] for i in range(0, len(values), 2)]
    return values[0]


def make_body(dp, fsdp):
    staged = dp == 8 and fsdp == 4

    def body(
        tokens, segments, cotangent, ln1_gain, ln1_bias, w_qkv, b_qkv, w_out, b_out,
        ln2_gain, ln2_bias, w_fc, b_fc, w_proj, b_proj, prefix_embed, w_mid, b_mid, w_kv, b_kv,
    ):
        depth = tokens.shape[1]
        half = depth // 2
        pairs = half // 128
        small = [ln1_gain, ln1_bias, b_out, ln2_gain, ln2_bias, b_proj, b_qkv, b_fc]
        widths = [one.shape[0] for one in small]
        shard_a = jnp.concatenate([w_qkv[:, i * depth : i * depth + half] for i in range(3)], 1)
        shard_b = jnp.concatenate(
            [w_qkv[:, i * depth + half : (i + 1) * depth] for i in range(3)] + [w_out], 1
        )
        if staged:
            order, order_f = place_order(dp, fsdp), direct_order(dp, fsdp)
            za, shard_b = fence(z_stage(shard_a, fsdp), shard_b)
            near, far = glue(*za)
            xa, zb, w_fc, small, segments, prefix_embed, w_proj = fence(
                first_stage(near, far, dp), z_stage(shard_b, fsdp), w_fc, small, segments,
                prefix_embed, w_proj,
            )
            xa, xb = join_stage(xa), glue(*zb)
            xa, xb, small = fence(xa, xb, small)
            ya = second_stage(*xa, dp)
            xb = first_stage(*xb, dp)
            zf = jnp.concatenate([w_fc[None], flip_z(w_fc[None], 2, fsdp)], 0)
            smalls = gather_small(small, dp * fsdp)
            proj = lax.all_gather(w_proj, AXES, axis=0, tiled=True)
        else:
            order = order_f = jnp.arange(PIECES, dtype=jnp.int32)
            smalls = gather_small(small, dp * fsdp)
            pieces_a, pieces_b, pieces_f = (natural_pieces(a) for a in (shard_a, shard_b, w_fc))
            proj = lax.all_gather(w_proj, AXES, axis=0, tiled=True)
        embed_pad = jnp.pad(prefix_embed, ((0, PADP - PREFIX), (0, 0)))
        vectors, bias_a, bias_b, fc_bias = unpack_call(smalls, widths, depth, w_fc.shape[1])
        mid_act, prefix_kv = adapter_call(embed_pad, w_mid, b_mid, w_kv, b_kv)
        edges = segment_edges(segments)
        if staged:
            ready = (order, edges, vectors, bias_a, bias_b, fc_bias, prefix_kv, mid_act)
            ya, xb, zf, ready = fence(ya, xb, zf, ready)
            order, edges, vectors, bias_a, bias_b, fc_bias, prefix_kv, mid_act = ready
            pieces_a = core_stage(ya, dp)
            yb = second_stage(*join_stage(xb), dp)
            far = flip_z(zf, 1, fsdp)
        hidden_a, sums_a, qkv_a, weight_a = front_call(
            order, edges, tokens, vectors, bias_a, prefix_kv, 0, pieces_a
        )
        if staged:
            hidden_a, yb, far = fence(hidden_a, yb, far)
            pieces_b = core_stage(yb, dp)
            own = jnp.concatenate([zf, far], 0)
            near_f = [own] + [flip_dp(own, m, dp) for m in (2, 4, 6)]
            across = flip_dp(own, 1, dp)
        hidden_b, sums_b, qkv_b, weight_b = front_call(
            order, edges, tokens, vectors, bias_b, prefix_kv, pairs, pieces_b
        )
        mixed, normed_two, gact, wout = out_call(
            order, tokens, hidden_a, hidden_b, vectors, cotangent, proj, pieces_b, 3 * half
        )
        if staged:
            mixed, near_f, across = fence(mixed, near_f, across)
            pieces_f = near_f + [across] + [flip_dp(one, 1, dp) for one in near_f[1:]]
        block_out, gmix, ghid = ffn_call(
            order_f, normed_two, gact, fc_bias, proj, mixed, cotangent, vectors, wout, pieces_f
        )
        total = prefix_call(
            (qkv_a, qkv_b), (sums_a, sums_b), (hidden_a, hidden_b), ghid, prefix_kv
        )
        if staged:
            total, ghid = fence(total, ghid)
            spread = [total] + [
                lax.ppermute(total, "fsdp", [(i, i ^ m) for i in range(fsdp)]) for m in (1, 2, 3)
            ]
        gqa, gka, gva = attend_backward(qkv_a, prefix_kv, edges, sums_a, hidden_a, ghid, 0)
        if staged:
            gqa, spread, ghid = fence(gqa, spread, ghid)
            total = tree_sum(spread)
            total, ghid = fence(total, ghid)
            spread = [total] + [flip_dp(total, m, dp) for m in (1, 2, 3)]
        gqb, gkb, gvb = attend_backward(qkv_b, prefix_kv, edges, sums_b, hidden_b, ghid, pairs)
        if staged:
            gqb, spread = fence(gqb, spread)
            total = tree_sum(spread)
            gqb, total = fence(gqb, total)
            other = flip_dp(total, 4, dp)
        else:
            total = lax.psum(total, AXES)
            other = jnp.zeros_like(total)
        grad_tokens = final_call(
            tokens, gmix, vectors, weight_a, weight_b, (gqa, gka, gva, gqb, gkb, gvb)
        )
        adapter = adapter_back_call(total, other, embed_pad, w_mid, w_kv, mid_act)
        return (block_out, grad_tokens) + adapter

    return body


def solution(mesh):
    dp, fsdp = mesh.shape["dp"], mesh.shape["fsdp"]
    rows, flat = P(AXES, None), P(AXES)
    return jax.shard_map(
        make_body(dp, fsdp),
        mesh=mesh,
        in_specs=(
            rows, flat, rows, flat, flat, rows, flat, rows, flat, flat, flat, rows, flat, rows,
            flat, P(), P(), P(), P(), P(),
        ),
        out_specs=(rows, rows, P(), P(), P(), P(), P()),
        check_vma=False,
    )
```
